32 devices in a mesh: shard: 8 (over y, x, core), ctx: 4 (over z).
Axes of the slice: x: 2, y: 2, z: 4, core: 2. Of those that a mesh axis runs over, the one named last changes fastest.
Arguments:
- tokens: bfloat16 [12288, 1600], P(('shard', 'ctx')), may hold values from -6 to 6
- cotangent: bfloat16 [12288, 1600], P(('shard', 'ctx')), may hold values from -12 to 12
- master_qkv: float32 [1600, 4800], P('shard', 'ctx'), may hold values from -0.15625 to 0.15625
- master_out: float32 [1600, 1600], P('shard', 'ctx'), may hold values from -2.5 to 2.5
- master_fc: float32 [1600, 6400], P('shard', 'ctx'), may hold values from -0.15625 to 0.15625
- master_proj: float32 [6400, 1600], P('shard', 'ctx'), may hold values from -0.078125 to 0.078125
- master_small: float32 [12, 1600], P(None, 'shard'), may hold values from -0.6 to 1.5, as said below
- first_qkv: float32 [1600, 4800], P('shard', 'ctx'), may hold values from -64 to 64
- first_out: float32 [1600, 1600], P('shard', 'ctx'), may hold values from -4 to 4
- first_fc: float32 [1600, 6400], P('shard', 'ctx'), may hold values from -28 to 28
- first_proj: float32 [6400, 1600], P('shard', 'ctx'), may hold values from -40 to 40
- first_small: float32 [12, 1600], P(None, 'shard'), may hold values from -64 to 64
- second_qkv: float32 [1600, 4800], P('shard', 'ctx'), may hold values from 12.288 to 49.152
- second_out: float32 [1600, 1600], P('shard', 'ctx'), may hold values from 0.0442368 to 0.1769472
- second_fc: float32 [1600, 6400], P('shard', 'ctx'), may hold values from 1.96608 to 7.86432
- second_proj: float32 [6400, 1600], P('shard', 'ctx'), may hold values from 4.42368 to 17.69472
- second_small: float32 [12, 1600], P(None, 'shard'), may hold values from 12.288 to 49.152
Outputs:
- output: bfloat16 [12288, 1600], P(('shard', 'ctx'))
- grad_input: float32 [12288, 1600], P(('shard', 'ctx'))
- master_qkv_new: float32 [1600, 4800], P('shard', 'ctx')
- master_out_new: float32 [1600, 1600], P('shard', 'ctx')
- master_fc_new: float32 [1600, 6400], P('shard', 'ctx')
- master_proj_new: float32 [6400, 1600], P('shard', 'ctx')
- master_small_new: float32 [12, 1600], P(None, 'shard')
- first_qkv_new: float32 [1600, 4800], P('shard', 'ctx')
- first_out_new: float32 [1600, 1600], P('shard', 'ctx')
- first_fc_new: float32 [1600, 6400], P('shard', 'ctx')
- first_proj_new: float32 [6400, 1600], P('shard', 'ctx')
- first_small_new: float32 [12, 1600], P(None, 'shard')
- second_qkv_new: float32 [1600, 4800], P('shard', 'ctx')
- second_out_new: float32 [1600, 1600], P('shard', 'ctx')
- second_fc_new: float32 [1600, 6400], P('shard', 'ctx')
- second_proj_new: float32 [6400, 1600], P('shard', 'ctx')
- second_small_new: float32 [12, 1600], P(None, 'shard')
- copy_qkv: bfloat16 [1600, 4800], P('shard', 'ctx')
- copy_out: bfloat16 [1600, 1600], P('shard', 'ctx')
- copy_fc: bfloat16 [1600, 6400], P('shard', 'ctx')
- copy_proj: bfloat16 [6400, 1600], P('shard', 'ctx')
- copy_small: bfloat16 [12, 1600], P(None, 'shard')
The draws below stay inside these ranges and needn't reach their ends.
Inputs may be any that keep to these rules, and one draw needn't show every extreme that they name: `master_small`: rows 0 and 2 (norm gains) lie in 0.5 to 1.5, the other rows in -0.6 to 0.6.
All inputs are finite; a program needn't handle non-finite values.
Results may differ from the reference program's by a relative error of at most 0.009.
The reference program's roundings to bfloat16 on the way count: a program that leaves them out, or rounds other values in their place, can miss the bound.
Values may be sent and summed in bfloat16 or wider, within the bound.
A program may use at most 384 MiB of HBM per device.

```python
import math
import jax
import jax.numpy as jnp
from jax import lax

D = 1600
HEADS = 25
HD = 64
FF = 6400
BLK = 128
PROMPT = 1024
CONT_DEV = 1
STEP = 10
PP = 256
ROWS_DEV = 384
GROUPS = 8
TOKENS = 12288
SMALL_ROWS = 12
N_CTX = 4


def draw_master_small(key, part):
    gain_key, shift_key = jax.random.split(jax.random.fold_in(key, 17))
    gains = jax.random.uniform(gain_key, (SMALL_ROWS, D), jnp.float32, 0.5, 1.5)
    shifts = jax.random.uniform(shift_key, (SMALL_ROWS, D), jnp.float32, -0.6, 0.6)
    row_index = jnp.arange(SMALL_ROWS)[:, None]
    is_gain = (row_index == 0) | (row_index == 2)
    return jnp.where(is_gain, gains, shifts).astype(jnp.float32)


def spiked(entries, rng, source, target, blocks, factor):
    owner, partner = [(jnp.arange(entries.shape[axis_at]) // (entries.shape[axis_at] // blocks)).reshape([-1 if axis == axis_at else 1 for axis in range(entries.ndim)]) for axis_at in (source, target)]
    chosen = jax.random.permutation(rng, blocks)[partner]
    strong = (owner == chosen) | (owner == (partner + blocks // 2) % blocks)
    return jnp.where(strong, factor * entries, entries)


def shard_levels(key, extent, cuts, least, high):
    gain = 1.0
    for dim, blocks in cuts:
        heights = jax.random.uniform(jax.random.fold_in(jax.random.fold_in(key, 6), dim), (blocks,), jnp.float32, least / len(cuts), high / len(cuts))
        gain = gain * jnp.repeat(jnp.exp(heights), extent[dim] // blocks).reshape((-1,) + (1,) * (len(extent) - 1 - dim))
    return gain


def noise(own_key, shape, width, bound, shards=(), kind=jnp.bfloat16):
    result = width * jax.random.normal(own_key, shape, jnp.float32)
    if shards:
        result = result * shard_levels(own_key, shape, shards, -0.22, 0.18)
    return jnp.clip(result, -bound, bound).astype(kind)


def noise_with(own_key, dims, scale, reach, cuts, heavy, kind=jnp.bfloat16):
    array = scale * jax.random.normal(own_key, dims, jnp.float32)
    if cuts:
        array = array * shard_levels(own_key, dims, cuts, -0.22, 0.18)
    return jnp.clip(spiked(array, jax.random.fold_in(own_key, 3), *heavy), -reach, reach).astype(kind)


def setup_inputs(seed: int = 0) -> dict:
    seeds = jax.random.split(jax.random.key(seed), 18)
    tokens = noise(seeds[0], (TOKENS, D), 1.0, 6.0, ((0, 32),))
    cotangent = noise_with(seeds[1], (TOKENS, D), 1.0, 12.0, ((0, 32),), (0, 1, 32, 2.75))
    master_qkv = noise(seeds[2], (D, 3 * D), D ** -0.5, 0.15625, ((0, 8), (1, 4)), jnp.float32)
    master_out = noise(seeds[3], (D, D), (max(D // 256, 1)) ** -0.5, 2.5, ((0, 8), (1, 4)), jnp.float32)
    master_fc = noise(seeds[4], (D, FF), D ** -0.5, 0.15625, ((0, 8), (1, 4)), jnp.float32)
    master_proj = noise(seeds[5], (FF, D), FF ** -0.5, 0.078125, ((0, 8), (1, 4)), jnp.float32)
    master_small = draw_master_small(jax.random.fold_in(seeds[17], 71), 0)
    first_qkv = noise(seeds[7], (D, 3 * D), (0.11 * TOKENS ** 0.5), 64.0, ((0, 8), (1, 4)), jnp.float32)
    first_out = noise(seeds[8], (D, D), (0.0066 * TOKENS ** 0.5), 4.0, ((0, 8), (1, 4)), jnp.float32)
    first_fc = noise(seeds[9], (D, FF), (0.044 * TOKENS ** 0.5), 28.0, ((0, 8), (1, 4)), jnp.float32)
    first_proj = noise(seeds[10], (FF, D), (0.066 * TOKENS ** 0.5), 40.0, ((0, 8), (1, 4)), jnp.float32)
    first_small = noise(seeds[11], (SMALL_ROWS, D), (0.11 * TOKENS ** 0.5), 64.0, ((1, 8),), jnp.float32)
    second_qkv = jnp.clip(jnp.exp(math.log(49.152) - 1.3862944 * jax.random.uniform(seeds[12], (D, 3 * D), jnp.float32) ** shard_levels(seeds[12], (D, 3 * D), ((0, 8), (1, 4)), -0.2, 0.2)), 12.288, 49.152)
    second_out = jnp.clip(jnp.exp(math.log(0.1769472) - 1.3862944 * jax.random.uniform(seeds[13], (D, D), jnp.float32) ** shard_levels(seeds[13], (D, D), ((0, 8), (1, 4)), -0.2, 0.2)), 0.0442368, 0.1769472)
    second_fc = jnp.clip(jnp.exp(math.log(7.86432) - 1.3862944 * jax.random.uniform(seeds[14], (D, FF), jnp.float32) ** shard_levels(seeds[14], (D, FF), ((0, 8), (1, 4)), -0.2, 0.2)), 1.96608, 7.86432)
    second_proj = jnp.clip(jnp.exp(math.log(17.69472) - 1.3862944 * jax.random.uniform(seeds[15], (FF, D), jnp.float32) ** shard_levels(seeds[15], (FF, D), ((0, 8), (1, 4)), -0.2, 0.2)), 4.42368, 17.69472)
    second_small = jnp.clip(jnp.exp(math.log(49.152) - 1.3862944 * jax.random.uniform(seeds[16], (SMALL_ROWS, D), jnp.float32) ** shard_levels(seeds[16], (SMALL_ROWS, D), ((1, 8),), -0.2, 0.2)), 12.288, 49.152)
    return {"tokens": tokens, "cotangent": cotangent, "master_qkv": master_qkv, "master_out": master_out, "master_fc": master_fc, "master_proj": master_proj, "master_small": master_small, "first_qkv": first_qkv, "first_out": first_out, "first_fc": first_fc, "first_proj": first_proj, "first_small": first_small, "second_qkv": second_qkv, "second_out": second_out, "second_fc": second_fc, "second_proj": second_proj, "second_small": second_small}


@jax.custom_vjp
def low(v):
    return lax.optimization_barrier(v.astype(jnp.bfloat16)).astype(jnp.float32)

@jax.custom_vjp
def low_back(v):
    return v

def low_keep(v):
    return (low(v), None)

def low_pass(kept, grad):
    return (grad,)

def back_keep(v):
    return (v, None)

def back_low(kept, grad):
    return (low(grad),)
low.defvjp(low_keep, low_pass)
low_back.defvjp(back_keep, back_low)
NORM_EPS = 1e-05
BETA_ONE = 0.9
BETA_TWO = 0.999
ADAM_EPS = 1e-08
WEIGHT_DECAY = 0.1
SMALL_RATE = 0.2
MASKED = -1e+30
HIGHEST = lax.Precision.HIGHEST

def norm_rows(values, gain_row, shift_row):
    row_mean = lax.optimization_barrier(jnp.mean(values, axis=-1, keepdims=True))
    centred = values - row_mean
    spread = lax.optimization_barrier(jnp.mean(centred * centred, axis=-1, keepdims=True))
    return centred * lax.rsqrt(spread + NORM_EPS) * gain_row + shift_row

def gelu_tanh(values):
    inner_arg = 0.7978845608028654 * (values + 0.044715 * values * values * values)
    return 0.5 * values * (1.0 + jnp.tanh(inner_arg))

def labels(ctx_index):
    places = jnp.arange(ROWS_DEV, dtype=jnp.int32)
    in_prompt = places < PP
    later = places - PP
    positions = jnp.where(in_prompt, ctx_index * PP + places, PROMPT + later % BLK)
    sequence = jnp.where(in_prompt, -1, ctx_index * CONT_DEV + later // BLK)
    return (positions.astype(jnp.int32), sequence.astype(jnp.int32))

def attend_block(queries, key_rows, value_rows, pos_query, seq_query, pos_key, seq_key):
    row_count = queries.shape[0]
    query_heads = queries.reshape(row_count, HEADS, HD)
    key_heads = key_rows.reshape(key_rows.shape[0], HEADS, HD)
    value_heads = value_rows.reshape(value_rows.shape[0], HEADS, HD)
    raw_scores = jnp.einsum('qhe,khe->hqk', query_heads, key_heads, precision=HIGHEST) * (1.0 / math.sqrt(HD))
    raw_scores = low_back(raw_scores)
    allowed = (pos_key[None, :] <= pos_query[:, None]) & ((seq_key[None, :] == -1) | (seq_key[None, :] == seq_query[:, None]))
    scores = jnp.where(allowed[None], raw_scores, MASKED)
    peak_score = lax.optimization_barrier(jnp.max(scores, axis=-1, keepdims=True))
    exp_scores = jnp.exp(scores - peak_score)
    softmax_probs = exp_scores / lax.optimization_barrier(jnp.sum(exp_scores, axis=-1, keepdims=True))
    attended = jnp.einsum('hqk,khe->qhe', low(softmax_probs), value_heads, precision=HIGHEST)
    return attended.reshape(row_count, D)

def group_layer(rows_in, w_qkv, w_out, w_fc, w_proj, small_params):
    act_one = low(norm_rows(rows_in, small_params[0], small_params[1]))
    qkv_bias = jnp.concatenate([small_params[4], jnp.zeros_like(small_params[4]), small_params[5]])
    qkv = low(low_back(jnp.dot(act_one, w_qkv, precision=HIGHEST) + qkv_bias))
    queries = qkv[:, :D]
    key_rows = qkv[:, D:2 * D]
    value_rows = qkv[:, 2 * D:]
    positions, sequence = jax.vmap(labels)(jnp.arange(N_CTX, dtype=jnp.int32))
    pos_key = positions.reshape(-1)
    seq_key = sequence.reshape(-1)
    attend = jax.checkpoint(attend_block)
    blocks = lax.map(lambda element: attend(element[0], key_rows, value_rows, element[1], element[2], pos_key, seq_key), (queries.reshape(N_CTX, ROWS_DEV, D), positions, sequence))
    attended = low(low_back(blocks.reshape(N_CTX * ROWS_DEV, D)))
    branch = low_back(jnp.dot(attended, w_out, precision=HIGHEST) + small_params[6])
    middle = rows_in + branch
    act_two = low(norm_rows(middle, small_params[2], small_params[3]))
    hidden = low_back(jnp.dot(act_two, w_fc, precision=HIGHEST) + small_params[7:7 + FF // D].reshape(FF))
    act_three = low(gelu_tanh(hidden))
    return middle + jnp.dot(act_three, w_proj, precision=HIGHEST) + small_params[SMALL_ROWS - 1]

def forward(inputs, masters):
    w_qkv = low(masters[0])
    w_out = low(masters[1])
    w_fc = low(masters[2])
    w_proj = low(masters[3])
    small_params = low(masters[4])
    group_step = jax.checkpoint(group_layer)

    def one_group(carried, rows_in):
        return (carried, group_step(rows_in, w_qkv, w_out, w_fc, w_proj, small_params))
    unused, outputs = lax.scan(one_group, jnp.float32(0.0), inputs.reshape(GROUPS, N_CTX * ROWS_DEV, D))
    return outputs.reshape(TOKENS, D)

def adamw(master, first, second, gradient, rate, decay):
    first_new = BETA_ONE * first + (1.0 - BETA_ONE) * gradient
    second_new = BETA_TWO * second + (1.0 - BETA_TWO) * gradient * gradient
    fix_one = 1.0 - BETA_ONE ** STEP
    fix_two = 1.0 - BETA_TWO ** STEP
    update = first_new / fix_one / (jnp.sqrt(second_new / fix_two) + ADAM_EPS)
    master_new = master - rate * (update + decay * master)
    return (master_new, first_new, second_new, master_new.astype(jnp.bfloat16))

def reference(tokens, cotangent, master_qkv, master_out, master_fc, master_proj, master_small, first_qkv, first_out, first_fc, first_proj, first_small, second_qkv, second_out, second_fc, second_proj, second_small):
    masters = (master_qkv, master_out, master_fc, master_proj, master_small)
    outputs, pullback = jax.vjp(forward, tokens.astype(jnp.float32), masters)
    grad_input, gradients = pullback(cotangent.astype(jnp.float32))
    rates = (D ** (-0.5), max(D // 256, 1) ** (-0.5), D ** (-0.5), FF ** (-0.5), SMALL_RATE)
    decays = (WEIGHT_DECAY, WEIGHT_DECAY, WEIGHT_DECAY, WEIGHT_DECAY, 0.0)
    firsts = (first_qkv, first_out, first_fc, first_proj, first_small)
    seconds = (second_qkv, second_out, second_fc, second_proj, second_small)
    results = [adamw(masters[index], firsts[index], seconds[index], gradients[index], rates[index], decays[index]) for index in range(5)]
    return (outputs.astype(jnp.bfloat16), grad_input, results[0][0], results[1][0], results[2][0], results[3][0], results[4][0], results[0][1], results[1][1], results[2][1], results[3][1], results[4][1], results[0][2], results[1][2], results[2][2], results[3][2], results[4][2], results[0][3], results[1][3], results[2][3], results[3][3], results[4][3])
```

```python
import functools
import math

import jax
import jax.numpy as jnp
from jax import lax
from jax.experimental import pallas as pl
from jax.experimental.pallas import tpu as pltpu
from jax.sharding import PartitionSpec as P

D = 1600
HD = 64
FF = 6400
BLK = 128
PROMPT = 1024
STEP = 10
TP = 4

NORM_EPS = 1e-05
BETA_ONE = 0.9
BETA_TWO = 0.999
ADAM_EPS = 1e-08
WEIGHT_DECAY = 0.1
SMALL_RATE = 0.2
MASKED = -1e30
MESH = pl.DeviceIdType.MESH
BF = jnp.bfloat16
F32 = jnp.float32
VMEM_BYTES = 60 * 1024 * 1024


def flip(index, mask):
    bit = 1
    while bit <= mask:
        if mask & bit:
            index = index + bit - 2 * bit * ((index // bit) % 2)
        bit *= 2
    return index


def spans(bits):
    tags = [0]
    for bit in bits:
        tags = tags + [t + bit for t in tags]
    return tags


def exchange_cost(us):
    return pl.CostEstimate(flops=0, bytes_accessed=us * 3_000_000, transcendentals=0)


def greet(peers):
    barrier = pltpu.get_barrier_semaphore()
    for peer in peers:
        pl.semaphore_signal(barrier, inc=1, device_id=peer, device_id_type=MESH)
    pl.semaphore_wait(barrier, len(peers))


def remote(src, dst, send, recv, peer):
    return pltpu.make_async_remote_copy(
        src_ref=src, dst_ref=dst, send_sem=send, recv_sem=recv, device_id=peer, device_id_type=MESH
    )


class Keep:
    def __init__(self, src, dst, room, sems):
        self.load = pltpu.make_async_copy(src, room, sems.at[0])
        self.store = pltpu.make_async_copy(room, dst, sems.at[1])
        self.load.start()

    def forward(self):
        self.load.wait()
        self.store.start()

    def finish(self):
        self.store.wait()


def add_into(target, other, rows):
    def step(i, carry):
        target[i] = (target[i].astype(F32) + other[i].astype(F32)).astype(BF)
        return carry

    lax.fori_loop(0, rows, step, 0)


def gather_kernel(ns, nc, *refs):
    srcs, column, dsts, columns, token = refs[:4], refs[4], refs[5:9], refs[9], refs[10]
    send, recv, send_z, recv_z, local_sem = refs[11:16]
    rooms, column_room = refs[16:20], refs[20]
    token[0] = jnp.int32(0)
    s, c = lax.axis_index("shard"), lax.axis_index("ctx")
    bits = [1 << k for k in range(1, ns.bit_length() - 1)]
    along = [(s, (c + j) % nc) for j in range(1, nc)]
    greet([(flip(s, b), c) for b in [1] + bits] + along)
    orders = [bits, bits, bits[::-1], bits[::-1]]

    def push(a, tag, bit):
        block = dsts[a].at[flip(s, tag)]
        got = tag + bit
        copy = remote(
            srcs[a] if tag == 0 else block, block, send.at[a, got], recv.at[a, got], (flip(s, bit), c)
        )
        copy.start()
        return copy

    def arrived(a, tag):
        block = dsts[a].at[flip(s, tag)]
        remote(block, block, send.at[a, tag], recv.at[a, tag], (s, c)).wait_recv()

    copies = []
    for k in range(len(bits)):
        for a in range(4):
            copies.append(push(a, 0, orders[a][k]))
    for a in range(4):
        copies.append(push(a, 0, 1))
    for j in range(1, nc):
        copy = remote(column, columns.at[c], send_z.at[j - 1], recv_z.at[j - 1], along[j - 1])
        copy.start()
        copies.append(copy)
    keep = [Keep(srcs[a], dsts[a].at[s], rooms[a], local_sem.at[a]) for a in range(4)]
    keep.append(Keep(column, columns.at[c], column_room, local_sem.at[4]))
    for own in keep:
        own.forward()
    for i in range(1, len(spans(bits))):
        for a in range(4):
            tag = spans(orders[a])[i]
            arrived(a, tag)
            last = max(k for k, b in enumerate(orders[a]) if tag & b)
            for b in orders[a][last + 1 :]:
                copies.append(push(a, tag, b))
            copies.append(push(a, tag, 1))
    for own in keep:
        own.finish()
    for a in range(4):
        for tag in spans(bits):
            arrived(a, tag + 1)
    for j in range(1, nc):
        block = columns.at[(c + nc - j) % nc]
        remote(block, block, send_z.at[j - 1], recv_z.at[j - 1], (s, c)).wait_recv()
    for copy in copies:
        copy.wait_send()


def gather_rows(blocks, column, ns, nc):
    any_spec = pl.BlockSpec(memory_space=pl.ANY)
    return pl.pallas_call(
        functools.partial(gather_kernel, ns, nc),
        out_shape=[jax.ShapeDtypeStruct((ns,) + b.shape, b.dtype) for b in blocks]
        + [jax.ShapeDtypeStruct((nc,) + column.shape, BF), jax.ShapeDtypeStruct((1,), jnp.int32)],
        in_specs=[any_spec] * 5,
        out_specs=[any_spec] * 5 + [pl.BlockSpec(memory_space=pltpu.SMEM)],
        scratch_shapes=[
            pltpu.SemaphoreType.DMA((4, ns)),
            pltpu.SemaphoreType.DMA((4, ns)),
            pltpu.SemaphoreType.DMA((nc - 1,)),
            pltpu.SemaphoreType.DMA((nc - 1,)),
            pltpu.SemaphoreType.DMA((5, 2)),
        ]
        + [pltpu.VMEM(b.shape, BF) for b in blocks]
        + [pltpu.VMEM(column.shape, BF)],
        compiler_params=pltpu.CompilerParams(collective_id=1, has_side_effects=True),
        cost_estimate=exchange_cost(95),
        name="gather_rows",
    )(*blocks, column)


def scatter_kernel(ns, n, *refs):
    grads, outs = refs[:n], refs[n : 2 * n]
    refs = refs[2 * n :]
    acc, got_core, got_late = refs[:n], refs[n : 2 * n], refs[2 * n : 3 * n]
    send_core, recv_core, send_late, recv_late, load_sem, out_sem = refs[3 * n :]
    s, c = lax.axis_index("shard"), lax.axis_index("ctx")
    bits = [1 << k for k in range(1, ns.bit_length() - 1)]
    nb = len(bits)
    greet([(flip(s, b), c) for b in [1] + bits])
    orders = [bits if a % 2 == 0 else bits[::-1] for a in range(n)]
    core_copies, loads, late = {}, {}, {}
    for i in range(ns // 2 - 1, -1, -1):
        for a in range(n):
            tag = spans(orders[a][::-1])[i]
            copy = remote(
                grads[a].at[flip(s, tag + 1)],
                got_core[a].at[tag // 2],
                send_core.at[a, tag // 2],
                recv_core.at[a, tag // 2],
                (flip(s, 1), c),
            )
            copy.start()
            core_copies[a, tag] = copy
            load = pltpu.make_async_copy(
                grads[a].at[flip(s, tag)], acc[a].at[tag // 2], load_sem.at[a, tag // 2]
            )
            load.start()
            loads[a, tag] = load
    def fold(a, tag, k):
        rows = acc[a].shape[1]
        if k == 0:
            loads[a, tag].wait()
            core_copies[a, tag].wait_recv()
            add_into(acc[a].at[tag // 2], got_core[a].at[tag // 2], rows)
        else:
            copy, slot = late[a, k - 1, tag]
            copy.wait_recv()
            add_into(acc[a].at[tag // 2], got_late[a].at[slot], rows)

    base = 0
    for k in range(nb):
        count = 2 ** (nb - 1 - k)
        for i in range(count - 1, -1, -1):
            for a in range(n):
                bit = orders[a][k]
                kept = spans(orders[a][k + 1 :][::-1])[i]
                fold(a, kept + bit, k)
                copy = remote(
                    acc[a].at[(kept + bit) // 2],
                    got_late[a].at[base + i],
                    send_late.at[a, base + i],
                    recv_late.at[a, base + i],
                    (flip(s, bit), c),
                )
                copy.start()
                late[a, k, kept] = (copy, base + i)
        for i in range(count - 1, -1, -1):
            for a in range(n):
                fold(a, spans(orders[a][k + 1 :][::-1])[i], k)
        base += count
    writes = []
    for a in range(n):
        fold(a, 0, nb)
        write = pltpu.make_async_copy(acc[a].at[0], outs[a], out_sem.at[a])
        write.start()
        writes.append(write)
    for copy in core_copies.values():
        copy.wait_send()
    for copy, _ in late.values():
        copy.wait_send()
    for write in writes:
        write.wait()


def scatter_rows(grads, ns):
    half = ns // 2
    n = len(grads)
    any_spec = pl.BlockSpec(memory_space=pl.ANY)
    return pl.pallas_call(
        functools.partial(scatter_kernel, ns, n),
        out_shape=[jax.ShapeDtypeStruct(g.shape[1:], BF) for g in grads],
        in_specs=[any_spec] * n,
        out_specs=[any_spec] * n,
        scratch_shapes=[pltpu.VMEM((half,) + g.shape[1:], BF) for g in grads]
        + [pltpu.VMEM((half,) + g.shape[1:], BF) for g in grads]
        + [pltpu.VMEM((half - 1,) + g.shape[1:], BF) for g in grads]
        + [
            pltpu.SemaphoreType.DMA((n, half)),
            pltpu.SemaphoreType.DMA((n, half)),
            pltpu.SemaphoreType.DMA((n, half - 1)),
            pltpu.SemaphoreType.DMA((n, half - 1)),
            pltpu.SemaphoreType.DMA((n, half)),
            pltpu.SemaphoreType.DMA((n,)),
        ],
        compiler_params=pltpu.CompilerParams(
            collective_id=2, has_side_effects=True, vmem_limit_bytes=VMEM_BYTES
        ),
        cost_estimate=exchange_cost(95),
        name="scatter_rows",
    )(*grads)


def quad_kernel(n, *refs):
    parts, passed, wide, passed_on = refs[:n], refs[n], refs[n + 1 : 2 * n + 1], refs[2 * n + 1]
    send, recv, local_sem = refs[2 * n + 2 : 2 * n + 5]
    rooms = refs[2 * n + 5 :]
    s, c = lax.axis_index("shard"), lax.axis_index("ctx")
    rank = s % TP
    greet([(flip(s, d), c) for d in (1, 2, 3)])
    copies = []
    keep = [Keep(passed, passed_on, rooms[n], local_sem.at[n])]
    for a in range(n):
        for d in (2, 3, 1):
            copy = remote(
                parts[a].at[flip(rank, d)], wide[a].at[rank], send.at[a, d], recv.at[a, d], (flip(s, d), c)
            )
            copy.start()
            copies.append(copy)
        keep.append(Keep(parts[a].at[rank], wide[a].at[rank], rooms[a], local_sem.at[a]))
    for own in keep:
        own.forward()
    for a in range(n):
        for d in (1, 2, 3):
            block = wide[a].at[flip(rank, d)]
            remote(block, block, send.at[a, d], recv.at[a, d], (s, c)).wait_recv()
    for own in keep:
        own.finish()
    for copy in copies:
        copy.wait_send()


def share_acts(acts, wide, send, recv, s, c, rank):
    copies = []

    def push(a, d, src):
        hop = 2 if d == 2 else 1
        copy = remote(
            src, wide[a].at[flip(rank, d - hop)], send.at[a, d], recv.at[a, d], (flip(s, hop), c)
        )
        copy.start()
        copies.append(copy)

    def arrived(a, d):
        block = wide[a].at[flip(rank, d)]
        remote(block, block, send.at[a, d], recv.at[a, d], (s, c)).wait_recv()

    for a in range(len(acts)):
        push(a, 2, acts[a])
        push(a, 1, acts[a])

    def finish():
        for a in range(len(acts)):
            arrived(a, 2)
            push(a, 3, wide[a].at[flip(rank, 2)])
        for a in range(len(acts)):
            arrived(a, 1)
            arrived(a, 3)
        for copy in copies:
            copy.wait_send()

    return finish


def share_quad(parts, passed, collective_id):
    any_spec = pl.BlockSpec(memory_space=pl.ANY)
    n = len(parts)
    return pl.pallas_call(
        functools.partial(quad_kernel, n),
        out_shape=[jax.ShapeDtypeStruct(p.shape, BF) for p in parts]
        + [jax.ShapeDtypeStruct(passed.shape, BF)],
        in_specs=[any_spec] * (n + 1),
        out_specs=[any_spec] * (n + 1),
        scratch_shapes=[
            pltpu.SemaphoreType.DMA((n, TP)),
            pltpu.SemaphoreType.DMA((n, TP)),
            pltpu.SemaphoreType.DMA((n + 1, 2)),
        ]
        + [pltpu.VMEM(p.shape[1:], BF) for p in parts]
        + [pltpu.VMEM(passed.shape, BF)],
        compiler_params=pltpu.CompilerParams(collective_id=collective_id, has_side_effects=True),
        cost_estimate=exchange_cost(30),
        name="share_quad",
    )(*parts, passed)


def share_kernel(ny, na, *refs):
    weight, acts, wide, wide_acts = refs[0], refs[1 : na + 1], refs[na + 1], refs[na + 2 : 2 * na + 2]
    send_far, recv_far, send_act, recv_act, local_sem = refs[2 * na + 2 : 2 * na + 7]
    rooms = refs[2 * na + 7 :]
    s, c = lax.axis_index("shard"), lax.axis_index("ctx")
    rank, y = s % TP, s // TP
    far = [(((y + j) % ny) * TP + rank, c) for j in range(1, ny)]
    greet([(flip(s, d), c) for d in (1, 2)] + far)
    finish = share_acts(acts, wide_acts, send_act, recv_act, s, c, rank)
    copies = []
    for j in range(1, ny):
        copy = remote(weight, wide.at[y], send_far.at[j - 1], recv_far.at[j - 1], far[j - 1])
        copy.start()
        copies.append(copy)
    keep = [Keep(weight, wide.at[y], rooms[na], local_sem.at[na])]
    for a in range(na):
        keep.append(Keep(acts[a], wide_acts[a].at[rank], rooms[a], local_sem.at[a]))
    for own in keep:
        own.forward()
    finish()
    for own in keep:
        own.finish()
    for j in range(1, ny):
        block = wide.at[(y + ny - j) % ny]
        remote(block, block, send_far.at[j - 1], recv_far.at[j - 1], (s, c)).wait_recv()
    for copy in copies:
        copy.wait_send()


def share_rows(weight, acts, ny):
    any_spec = pl.BlockSpec(memory_space=pl.ANY)
    na = len(acts)
    return pl.pallas_call(
        functools.partial(share_kernel, ny, na),
        out_shape=[jax.ShapeDtypeStruct((ny,) + weight.shape, BF)]
        + [jax.ShapeDtypeStruct((TP,) + act.shape, BF) for act in acts],
        in_specs=[any_spec] * (na + 1),
        out_specs=[any_spec] * (na + 1),
        scratch_shapes=[
            pltpu.SemaphoreType.DMA((ny - 1,)),
            pltpu.SemaphoreType.DMA((ny - 1,)),
            pltpu.SemaphoreType.DMA((na, TP)),
            pltpu.SemaphoreType.DMA((na, TP)),
            pltpu.SemaphoreType.DMA((na + 1, 2)),
        ]
        + [pltpu.VMEM(act.shape, BF) for act in acts]
        + [pltpu.VMEM(weight.shape, BF)],
        compiler_params=pltpu.CompilerParams(
            collective_id=3, has_side_effects=True, vmem_limit_bytes=VMEM_BYTES
        ),
        cost_estimate=exchange_cost(60),
        name="share_rows",
    )(weight, *acts)


def return_kernel(ny, pieces, *refs):
    grad, acts = refs[0], refs[1:3]
    out, act_outs = refs[3], refs[4:6]
    part, got_far, act_part, act_core, act_far = refs[6:11]
    send_far, recv_far, send_act, recv_act, load_sem, act_load, out_sem, act_sem = refs[11:]
    s, c = lax.axis_index("shard"), lax.axis_index("ctx")
    rank, y = s % TP, s // TP
    far = [(((y + j) % ny) * TP + rank, c) for j in range(1, ny)]
    greet([(flip(s, d), c) for d in (1, 2)] + far)
    act_rows = act_part.shape[2]
    rows = part.shape[1]
    act_loads, act_copies = {}, {}
    for a in range(2):
        for d in (2, 0):
            copy = remote(
                acts[a].at[flip(rank, d + 1)],
                act_core.at[a, d // 2],
                send_act.at[a, d // 2],
                recv_act.at[a, d // 2],
                (flip(s, 1), c),
            )
            copy.start()
            act_copies[a, d] = copy
            load = pltpu.make_async_copy(
                acts[a].at[flip(rank, d)], act_part.at[a, d // 2], act_load.at[a, d // 2]
            )
            load.start()
            act_loads[a, d] = load
    far_copies, loads = {}, {}
    for p in range(pieces):
        for j in range(1, ny):
            copy = remote(
                grad.at[(y + j) % ny, p],
                got_far.at[p, j - 1],
                send_far.at[p, j - 1],
                recv_far.at[p, j - 1],
                far[j - 1],
            )
            copy.start()
            far_copies[p, j] = copy
        load = pltpu.make_async_copy(grad.at[y, p], part.at[p], load_sem.at[p])
        load.start()
        loads[p] = load
    writes = []

    def finish_act(a):
        act_copies[a, 3].wait_recv()
        add_into(act_part.at[a, 0], act_far.at[a], act_rows)
        write = pltpu.make_async_copy(act_part.at[a, 0], act_outs[a], act_sem.at[a])
        write.start()
        writes.append(write)

    for a in range(2):
        for d in (2, 0):
            act_loads[a, d].wait()
            act_copies[a, d].wait_recv()
            add_into(act_part.at[a, d // 2], act_core.at[a, d // 2], act_rows)
            if d == 2:
                copy = remote(
                    act_part.at[a, 1], act_far.at[a], send_act.at[a, 2], recv_act.at[a, 2], (flip(s, 2), c)
                )
                copy.start()
                act_copies[a, 3] = copy
    for p in range(pieces):
        loads[p].wait()
        for j in range(1, ny):
            far_copies[p, j].wait_recv()
            add_into(part.at[p], got_far.at[p, j - 1], rows)
        write = pltpu.make_async_copy(part.at[p], out.at[p], out_sem.at[p])
        write.start()
        writes.append(write)
        if p == pieces // 2:
            finish_act(0)
    finish_act(1)
    for write in writes:
        write.wait()
    for group in (act_copies, far_copies):
        for copy in group.values():
            copy.wait_send()


def return_grads(grad, acts):
    ny, pieces = grad.shape[:2]
    block = grad.shape[2:]
    act = acts[0].shape[1:]
    any_spec = pl.BlockSpec(memory_space=pl.ANY)
    return pl.pallas_call(
        functools.partial(return_kernel, ny, pieces),
        out_shape=[jax.ShapeDtypeStruct(grad.shape[1:], BF)]
        + [jax.ShapeDtypeStruct(act, BF) for _ in acts],
        in_specs=[any_spec] * 3,
        out_specs=[any_spec] * 3,
        scratch_shapes=[
            pltpu.VMEM((pieces,) + block, BF),
            pltpu.VMEM((pieces, ny - 1) + block, BF),
            pltpu.VMEM((2, 2) + act, BF),
            pltpu.VMEM((2, 2) + act, BF),
            pltpu.VMEM((2,) + act, BF),
            pltpu.SemaphoreType.DMA((pieces, ny - 1)),
            pltpu.SemaphoreType.DMA((pieces, ny - 1)),
            pltpu.SemaphoreType.DMA((2, 3)),
            pltpu.SemaphoreType.DMA((2, 3)),
            pltpu.SemaphoreType.DMA((pieces,)),
            pltpu.SemaphoreType.DMA((2, 2)),
            pltpu.SemaphoreType.DMA((pieces,)),
            pltpu.SemaphoreType.DMA((2,)),
        ],
        compiler_params=pltpu.CompilerParams(
            collective_id=4, has_side_effects=True, vmem_limit_bytes=VMEM_BYTES
        ),
        cost_estimate=exchange_cost(70),
        name="return_grads",
    )(grad, *acts)


NN = (((1,), (0,)), ((), ()))
NT = (((1,), (1,)), ((), ()))
TN = (((0,), (0,)), ((), ()))


def mm(left, right, dims):
    return lax.dot_general(left, right, dims, preferred_element_type=F32)


def halves(rows):
    lane = lax.broadcasted_iota(jnp.int32, (rows, 2 * HD), 1)
    return lane < HD


def one_of(values, low, head):
    return jnp.where(low if head == 0 else jnp.logical_not(low), values, jnp.zeros_like(values))


def for_pairs(width, body):
    pairs = width // (2 * HD)

    def step(i, carry):
        body(pl.ds(pl.multiple_of(i * 2 * HD, 2 * HD), 2 * HD), 2 * i, 2)
        return carry

    lax.fori_loop(0, pairs, step, 0)
    if width % (2 * HD):
        body(pl.ds(pairs * 2 * HD, HD), 2 * pairs, 1)


def attend_kernel(q_ref, k_ref, v_ref, bias_ref, o_ref, lse_ref):
    rows, width = q_ref.shape
    keys = k_ref.shape[0]
    low = halves(keys)

    def body(cols, first, count):
        q = q_ref[:, cols]
        k = k_ref[:, cols]
        v = v_ref[:, cols]
        total = None
        for head in range(count):
            k_h = one_of(k, low, head) if count == 2 else k
            v_h = one_of(v, low, head) if count == 2 else v
            scores = mm(q, k_h, NT) + bias_ref[...]
            peak = jnp.max(scores, axis=1, keepdims=True)
            weights = jnp.exp(scores - peak)
            norm = jnp.sum(weights, axis=1, keepdims=True)
            part = mm(weights.astype(BF), v_h, NN) / norm
            total = part if total is None else total + part
            lse_ref[first + head] = peak + jnp.log(norm)
        o_ref[:, cols] = total.astype(BF)

    for_pairs(width, body)


def attend_forward(q, k, v, bias):
    heads = q.shape[1] // HD
    return pl.pallas_call(
        attend_kernel,
        out_shape=[
            jax.ShapeDtypeStruct(q.shape, BF),
            jax.ShapeDtypeStruct((heads, q.shape[0], 1), F32),
        ],
        in_specs=[pl.BlockSpec(memory_space=pltpu.VMEM)] * 4,
        out_specs=[pl.BlockSpec(memory_space=pltpu.VMEM)] * 2,
        compiler_params=pltpu.CompilerParams(vmem_limit_bytes=VMEM_BYTES),
        cost_estimate=pl.CostEstimate(
            flops=16 * q.shape[0] * k.shape[0] * q.shape[1],
            bytes_accessed=20_000_000,
            transcendentals=q.shape[0] * k.shape[0] * heads,
        ),
        name="attend_forward",
    )(q, k, v, bias)


def attend_back_kernel(q_ref, k_ref, v_ref, g_ref, lse_ref, bias_ref, _, dq_ref, dk_ref, dv_ref):
    rows, width = q_ref.shape
    keys = k_ref.shape[0]
    low_q = halves(rows)
    low_k = halves(keys)
    scale = 1.0 / math.sqrt(HD)

    def body(cols, first, count):
        q = q_ref[:, cols]
        k = k_ref[:, cols]
        v = v_ref[:, cols]
        g = g_ref[:, cols]
        dq = dk = dv = None
        for head in range(count):
            if count == 2:
                q_h, g_h = one_of(q, low_q, head), one_of(g, low_q, head)
                k_h = one_of(k, low_k, head)
            else:
                q_h, g_h, k_h = q, g, k
            scores = mm(k, q_h, NT) + bias_ref[...]
            probs = jnp.exp(scores - lse_ref[first + head])
            grad = mm(v, g_h, NT)
            both = probs * grad
            centre = jnp.sum(both, axis=0, keepdims=True)
            ds = (both - probs * centre).astype(BF)
            dq_h = mm(ds, k_h, TN)
            dk_h = mm(ds, q_h, NN)
            dv_h = mm(probs.astype(BF), g_h, NN)
            dq = dq_h if dq is None else dq + dq_h
            dk = dk_h if dk is None else dk + dk_h
            dv = dv_h if dv is None else dv + dv_h
        dq_ref[:, cols] = (dq * scale).astype(BF)
        dk_ref[:, cols] = dk.astype(BF)
        dv_ref[:, cols] = dv.astype(BF)

    for_pairs(width, body)


def attend_backward(q, k, v, g, lse, bias, ready):
    heads = q.shape[1] // HD
    return pl.pallas_call(
        attend_back_kernel,
        out_shape=[jax.ShapeDtypeStruct(x.shape, BF) for x in (q, k, v)],
        in_specs=[pl.BlockSpec(memory_space=pltpu.VMEM)] * 6 + [pl.BlockSpec(memory_space=pl.ANY)],
        out_specs=[pl.BlockSpec(memory_space=pltpu.VMEM)] * 3,
        compiler_params=pltpu.CompilerParams(vmem_limit_bytes=VMEM_BYTES),
        cost_estimate=pl.CostEstimate(
            flops=40 * q.shape[0] * k.shape[0] * q.shape[1],
            bytes_accessed=30_000_000,
            transcendentals=q.shape[0] * k.shape[0] * heads,
        ),
        name="attend_backward",
    )(q, k, v, g, lse, bias, ready)


def normed(values):
    mean = jnp.mean(values, axis=-1, keepdims=True)
    centred = values - mean
    spread = jnp.mean(centred * centred, axis=-1, keepdims=True)
    inverse = lax.rsqrt(spread + NORM_EPS)
    return centred * inverse, inverse


def norm_back(u, unit, inverse, gain):
    gu = gain * u
    grad = inverse * (
        gu - jnp.mean(gu, axis=-1, keepdims=True) - unit * jnp.mean(gu * unit, axis=-1, keepdims=True)
    )
    return grad, jnp.sum(u * unit, axis=0), jnp.sum(u, axis=0)


def adamw(master, first, second, gradient, rate, decay):
    first_new = BETA_ONE * first + (1.0 - BETA_ONE) * gradient
    second_new = BETA_TWO * second + (1.0 - BETA_TWO) * gradient * gradient
    fix_one = 1.0 - BETA_ONE**STEP
    fix_two = 1.0 - BETA_TWO**STEP
    update = first_new / fix_one / (jnp.sqrt(second_new / fix_two) + ADAM_EPS)
    master_new = master - rate * (update + decay * master)
    return (master_new, first_new, second_new, master_new.astype(BF))


def behind(token, value):
    return jnp.where(token[0] == 0, value, jnp.zeros_like(value))


def local(
    tokens,
    cotangent,
    master_qkv,
    master_out,
    master_fc,
    master_proj,
    master_small,
    first_qkv,
    first_out,
    first_fc,
    first_proj,
    first_small,
    second_qkv,
    second_out,
    second_fc,
    second_proj,
    second_small,
):
    ns, nc = lax.axis_size("shard"), lax.axis_size("ctx")
    s, c = lax.axis_index("shard"), lax.axis_index("ctx")
    ny = ns // TP
    rank = s % TP
    rows = tokens.shape[0]
    prompt_rows = PROMPT // nc
    kr = D // ns
    hs = FF // ns // TP
    hq = ns * hs
    hc = hq // nc
    pack = 8 if kr % 8 == 0 else 4
    packed = (kr // pack, pack, D)
    act_pack = (rows // 8, 8, D)
    far_groups = [[y * TP + r for y in range(ny)] for r in range(TP)]

    qc = master_qkv.shape[1]
    attn_block = jnp.concatenate([master_qkv.astype(BF), master_out.astype(BF)], axis=1)
    attn_z = lax.all_gather(attn_block, "ctx", axis=0)
    small_all = lax.all_gather(master_small.astype(BF), "shard", axis=0)
    small = small_all.transpose(1, 0, 2).reshape(master_small.shape[0], D).astype(F32)
    fc_parts = master_fc.astype(BF).reshape(kr, ns // nc, TP, hs).transpose(2, 0, 1, 3)
    proj_parts = master_proj.astype(BF).reshape(TP, hs, D // nc)
    fc_quad, proj_quad, prompt_own = share_quad(
        [fc_parts.reshape(TP, kr, hc), proj_parts], tokens[:prompt_rows], 5
    )
    prompt_tokens = lax.all_gather(prompt_own, "ctx", axis=0, tiled=True)
    fc_z = lax.all_gather(lax.optimization_barrier((attn_z, fc_quad))[1], "ctx", axis=0)

    qkv_rows = attn_z[:, :, :qc].transpose(1, 0, 2).reshape(kr, 3, D)
    out_rows = attn_z[:, :, qc:].transpose(1, 0, 2).reshape(packed)
    gathered = gather_rows(
        [qkv_rows[:, i].reshape(packed) for i in range(3)] + [out_rows], proj_quad, ns, nc
    )
    w_q, w_k, w_v, w_o = [w.reshape(D, D) for w in gathered[:4]]
    proj_z = gathered[4]
    fc_z = behind(gathered[5], fc_z).reshape(nc, TP, kr, hc)
    fc_rows = fc_z.transpose(1, 2, 0, 3).reshape((TP * packed[0],) + packed[1:2] + (hq,))
    proj_rows = proj_z.transpose(1, 2, 0, 3).reshape(TP * hs, D)
    proj_wide = lax.all_gather(
        proj_rows, "shard", axis=0, tiled=True, axis_index_groups=far_groups
    )

    own = tokens.astype(F32)
    unit_one, inverse_one = normed(own)
    all_rows = jnp.concatenate([prompt_tokens, tokens[prompt_rows:]], axis=0).astype(F32)
    unit_all = normed(all_rows)[0]
    act_all = (unit_all * small[0] + small[1]).astype(BF)
    act_one = jnp.concatenate(
        [lax.dynamic_slice_in_dim(act_all, c * prompt_rows, prompt_rows), act_all[PROMPT:]], axis=0
    )
    scale = 1.0 / math.sqrt(HD)
    q = (mm(act_one, w_q, NN) + small[4]).astype(BF) * BF(scale)
    k = mm(act_all, w_k, NN).astype(BF)
    v = (mm(act_all, w_v, NN) + small[5]).astype(BF)
    places = jnp.arange(rows, dtype=jnp.int32)
    in_prompt = places < prompt_rows
    later = places - prompt_rows
    pos_query = jnp.where(in_prompt, c * prompt_rows + places, PROMPT + later % BLK)
    seq_query = jnp.where(in_prompt, -1, later // BLK)
    cont_keys = jnp.arange(rows - prompt_rows, dtype=jnp.int32)
    pos_key = jnp.concatenate([jnp.arange(PROMPT, dtype=jnp.int32), PROMPT + cont_keys % BLK])
    seq_key = jnp.concatenate([jnp.full((PROMPT,), -1, jnp.int32), cont_keys // BLK])
    allowed = (pos_key[None, :] <= pos_query[:, None]) & (
        (seq_key[None, :] == -1) | (seq_key[None, :] == seq_query[:, None])
    )
    bias = jnp.where(allowed, 0.0, MASKED).astype(F32)
    attended, log_totals = attend_forward(q, k, v, bias)
    middle = own + mm(attended, w_o, NN) + small[6]
    unit_two, inverse_two = normed(middle)
    act_two = (unit_two * small[2] + small[3]).astype(BF)

    fc_wide, act_wide, cot_wide = share_rows(
        fc_rows, [act_two.reshape(act_pack), cotangent.reshape(act_pack)], ny
    )
    w_fc = fc_wide.reshape(D, hq)
    w_proj = proj_wide
    act_wide = act_wide.reshape(TP * rows, D)
    cot_wide = cot_wide.reshape(TP * rows, D)
    fc_bias = lax.dynamic_index_in_dim(
        small[7 : 7 + FF // D].reshape(ns, TP, hs), rank, axis=1, keepdims=False
    ).reshape(hq)
    hidden = mm(act_wide, w_fc, NN) + fc_bias
    cube = 0.7978845608028654 * (hidden + 0.044715 * hidden * hidden * hidden)
    bent = jnp.tanh(cube)
    act_three = (0.5 * hidden * (1.0 + bent)).astype(BF)
    slope = 0.5 * (1.0 + bent) + 0.5 * hidden * (1.0 - bent * bent) * 0.7978845608028654 * (
        1.0 + 3.0 * 0.044715 * hidden * hidden
    )
    grad_hidden = (mm(cot_wide, w_proj, NT) * slope).astype(BF)
    grad_proj = mm(act_three, cot_wide, TN).astype(BF)
    proj_far = lax.psum_scatter(
        grad_proj, "shard", scatter_dimension=0, tiled=True, axis_index_groups=far_groups
    )
    out_part = mm(act_three, w_proj, NN).astype(BF)
    mid_part = mm(grad_hidden, w_fc, NT).astype(BF)
    grad_fc = mm(act_wide, grad_hidden, TN).astype(BF)
    grad_fc_bias = jnp.sum(grad_hidden, axis=0, dtype=F32)
    fc_far, mid_sum, out_sum = return_grads(
        grad_fc.reshape((ny, TP) + packed),
        [mid_part.reshape((TP,) + act_pack), out_part.reshape((TP,) + act_pack)],
    )
    output = middle + out_sum.reshape(rows, D).astype(F32) + small[small.shape[0] - 1]
    proj_far = proj_far.reshape(TP * hs, nc, D // nc).transpose(1, 0, 2)
    proj_near = lax.psum_scatter(proj_far, "ctx", scatter_dimension=0)
    fc_far = fc_far.reshape(TP * kr, nc, hc).transpose(1, 0, 2)
    fc_near = lax.psum_scatter(fc_far, "ctx", scatter_dimension=0)

    grad_output = cotangent.astype(F32)
    grad_norm, gain_two, shift_two = norm_back(
        mid_sum.reshape(rows, D).astype(F32), unit_two, inverse_two, small[2]
    )
    grad_middle = grad_output + grad_norm
    grad_branch = grad_middle.astype(BF)
    grad_wo = mm(attended, grad_branch, TN).astype(BF)
    grad_attended = mm(grad_branch, w_o, NT).astype(BF)
    grad_q, grad_k, grad_v = attend_backward(
        q, k, v, grad_attended, log_totals.transpose(0, 2, 1), bias.T, proj_far
    )
    key_part = mm(grad_k, w_k, NT) + mm(grad_v, w_v, NT)
    prompt_sum = lax.psum_scatter(
        key_part[:PROMPT].astype(BF), "ctx", scatter_dimension=0, tiled=True
    )
    query_part = mm(grad_q, w_q, NT)
    grad_wq = mm(act_one, grad_q, TN).astype(BF)
    grad_wk = mm(act_all, grad_k, TN).astype(BF)
    grad_wv = mm(act_all, grad_v, TN).astype(BF)

    hidden_grads = lax.dynamic_update_index_in_dim(
        jnp.zeros((ns, TP, hs), F32), grad_fc_bias.reshape(ns, 1, hs), rank, axis=1
    )
    small_grads = jnp.concatenate(
        [
            jnp.stack(
                [
                    jnp.sum(key_part * unit_all, axis=0) + jnp.sum(query_part * unit_one, axis=0),
                    jnp.sum(key_part, axis=0) + jnp.sum(query_part, axis=0),
                    gain_two,
                    shift_two,
                    jnp.sum(grad_q, axis=0, dtype=F32),
                    jnp.sum(grad_v, axis=0, dtype=F32),
                    jnp.sum(grad_branch, axis=0, dtype=F32),
                ]
            ),
            hidden_grads.reshape(FF // D, D),
            jnp.sum(grad_output, axis=0)[None],
        ],
        axis=0,
    )
    n_small = small_grads.shape[0]
    small_parts = small_grads.reshape(n_small, ns, kr).transpose(1, 0, 2).reshape(ns, n_small * kr)
    small_parts = jnp.pad(small_parts, ((0, 0), (0, 8 * D - n_small * kr)))
    back_q, back_k, back_v, back_o, back_small = scatter_rows(
        [g.reshape((ns,) + packed) for g in (grad_wq, grad_wk, grad_wv, grad_wo)]
        + [small_parts.astype(BF).reshape(ns, 1, 8, D)],
        ns,
    )
    fc_back, proj_back, _ = share_quad(
        [fc_near.reshape(TP, kr, hc), proj_near.reshape(TP, hs, D // nc)], back_small, 6
    )
    qkv_back = jnp.concatenate([b.reshape(kr, D) for b in (back_q, back_k, back_v)], axis=1)
    attn_back = jnp.concatenate(
        [qkv_back.reshape(kr, nc, qc), back_o.reshape(kr, nc, D // nc)], axis=2
    ).transpose(1, 0, 2)
    wide_rows = attn_back.shape[2]
    small_back = back_small.reshape(8 * D)[: 8 * wide_rows].reshape(1, 8, wide_rows)
    grad_attn = lax.psum_scatter(
        jnp.concatenate([attn_back, jnp.broadcast_to(small_back, (nc, 8, wide_rows))], axis=1),
        "ctx",
        scatter_dimension=0,
    )
    small_own = grad_attn[kr:].reshape(-1)[: n_small * kr].reshape(n_small, kr).astype(F32)
    grad_act = query_part + jnp.concatenate(
        [prompt_sum.astype(F32), key_part[PROMPT:]], axis=0
    )
    grad_norm, _, _ = norm_back(grad_act, unit_one, inverse_one, small[0])
    grad_input = grad_middle + grad_norm

    gradients = (
        grad_attn[:kr, :qc].astype(F32),
        grad_attn[:kr, qc:].astype(F32),
        fc_back.reshape(TP, kr, ns // nc, hs).transpose(1, 2, 0, 3).reshape(kr, FF // nc).astype(F32),
        proj_back.reshape(TP * hs, D // nc).astype(F32),
        small_own,
    )
    masters = (master_qkv, master_out, master_fc, master_proj, master_small)
    firsts = (first_qkv, first_out, first_fc, first_proj, first_small)
    seconds = (second_qkv, second_out, second_fc, second_proj, second_small)
    rates = (D ** (-0.5), max(D // 256, 1) ** (-0.5), D ** (-0.5), FF ** (-0.5), SMALL_RATE)
    decays = (WEIGHT_DECAY, WEIGHT_DECAY, WEIGHT_DECAY, WEIGHT_DECAY, 0.0)
    results = [
        adamw(masters[i], firsts[i], seconds[i], gradients[i], rates[i], decays[i]) for i in range(5)
    ]
    return (output.astype(BF), grad_input) + tuple(results[i][j] for j in range(4) for i in range(5))


def solution(mesh):
    row_spec = P(("shard", "ctx"), None)
    weight_specs = (P("shard", "ctx"),) * 4 + (P(None, "shard"),)
    return jax.shard_map(
        local,
        mesh=mesh,
        in_specs=(row_spec, row_spec) + weight_specs * 3,
        out_specs=(row_spec, row_spec) + weight_specs * 4,
        check_vma=False,
    )
```

```python
import functools
import math

import jax
import jax.numpy as jnp
from jax import lax
from jax.experimental import pallas as pl
from jax.experimental.pallas import tpu as pltpu
from jax.sharding import PartitionSpec as P

D = 1600
HD = 64
FF = 6400
BLK = 128
PROMPT = 1024
STEP = 10
TP = 4

NORM_EPS = 1e-05
BETA_ONE = 0.9
BETA_TWO = 0.999
ADAM_EPS = 1e-08
WEIGHT_DECAY = 0.1
SMALL_RATE = 0.2
MASKED = -1e30
MESH = pl.DeviceIdType.MESH
BF = jnp.bfloat16
F32 = jnp.float32
VMEM_BYTES = 60 * 1024 * 1024


def flip(index, mask):
    bit = 1
    while bit <= mask:
        if mask & bit:
            index = index + bit - 2 * bit * ((index // bit) % 2)
        bit *= 2
    return index


def spans(bits):
    tags = [0]
    for bit in bits:
        tags = tags + [t + bit for t in tags]
    return tags


def exchange_cost(us):
    return pl.CostEstimate(flops=0, bytes_accessed=us * 3_000_000, transcendentals=0)


def greet(peers):
    barrier = pltpu.get_barrier_semaphore()
    for peer in peers:
        pl.semaphore_signal(barrier, inc=1, device_id=peer, device_id_type=MESH)
    pl.semaphore_wait(barrier, len(peers))


def remote(src, dst, send, recv, peer):
    return pltpu.make_async_remote_copy(
        src_ref=src, dst_ref=dst, send_sem=send, recv_sem=recv, device_id=peer, device_id_type=MESH
    )


class Keep:
    def __init__(self, src, dst, room, sems):
        self.load = pltpu.make_async_copy(src, room, sems.at[0])
        self.store = pltpu.make_async_copy(room, dst, sems.at[1])
        self.load.start()

    def forward(self):
        self.load.wait()
        self.store.start()

    def finish(self):
        self.store.wait()


def add_into(target, other, rows):
    def step(i, carry):
        target[i] = (target[i].astype(F32) + other[i].astype(F32)).astype(BF)
        return carry

    lax.fori_loop(0, rows, step, 0)


def gather_kernel(ns, *refs):
    srcs, dsts, token = refs[:4], refs[4:8], refs[8]
    send, recv, local_sem = refs[9:12]
    rooms = refs[12:]
    token[0] = jnp.int32(0)
    s, c = lax.axis_index("shard"), lax.axis_index("ctx")
    bits = [1 << k for k in range(1, ns.bit_length() - 1)]
    greet([(flip(s, b), c) for b in [1] + bits])
    orders = [bits, bits, bits[::-1], bits[::-1]]

    def push(a, tag, bit):
        block = dsts[a].at[flip(s, tag)]
        got = tag + bit
        copy = remote(
            srcs[a] if tag == 0 else block, block, send.at[a, got], recv.at[a, got], (flip(s, bit), c)
        )
        copy.start()
        return copy

    def arrived(a, tag):
        block = dsts[a].at[flip(s, tag)]
        remote(block, block, send.at[a, tag], recv.at[a, tag], (s, c)).wait_recv()

    copies = []
    for k in range(len(bits)):
        for a in range(4):
            copies.append(push(a, 0, orders[a][k]))
    for a in range(4):
        copies.append(push(a, 0, 1))
    keep = [Keep(srcs[a], dsts[a].at[s], rooms[a], local_sem.at[a]) for a in range(4)]
    for own in keep:
        own.forward()
    for i in range(1, len(spans(bits))):
        for a in range(4):
            tag = spans(orders[a])[i]
            arrived(a, tag)
            last = max(k for k, b in enumerate(orders[a]) if tag & b)
            for b in orders[a][last + 1 :]:
                copies.append(push(a, tag, b))
            copies.append(push(a, tag, 1))
    for own in keep:
        own.finish()
    for a in range(4):
        for tag in spans(bits):
            arrived(a, tag + 1)
    for copy in copies:
        copy.wait_send()


def gather_rows(blocks, ns):
    any_spec = pl.BlockSpec(memory_space=pl.ANY)
    return pl.pallas_call(
        functools.partial(gather_kernel, ns),
        out_shape=[jax.ShapeDtypeStruct((ns,) + b.shape, b.dtype) for b in blocks]
        + [jax.ShapeDtypeStruct((1,), jnp.int32)],
        in_specs=[any_spec] * 4,
        out_specs=[any_spec] * 4 + [pl.BlockSpec(memory_space=pltpu.SMEM)],
        scratch_shapes=[
            pltpu.SemaphoreType.DMA((4, ns)),
            pltpu.SemaphoreType.DMA((4, ns)),
            pltpu.SemaphoreType.DMA((4, 2)),
        ]
        + [pltpu.VMEM(b.shape, BF) for b in blocks],
        compiler_params=pltpu.CompilerParams(collective_id=1, has_side_effects=True),
        cost_estimate=exchange_cost(95),
        name="gather_rows",
    )(*blocks)


def scatter_kernel(ns, n, *refs):
    grads, outs = refs[:n], refs[n : 2 * n]
    refs = refs[2 * n :]
    acc, got_core, got_late = refs[:n], refs[n : 2 * n], refs[2 * n : 3 * n]
    send_core, recv_core, send_late, recv_late, load_sem, out_sem = refs[3 * n :]
    s, c = lax.axis_index("shard"), lax.axis_index("ctx")
    bits = [1 << k for k in range(1, ns.bit_length() - 1)]
    nb = len(bits)
    greet([(flip(s, b), c) for b in [1] + bits])
    orders = [bits if a % 2 == 0 else bits[::-1] for a in range(n)]
    core_copies, loads, late = {}, {}, {}
    for i in range(ns // 2 - 1, -1, -1):
        for a in range(n):
            tag = spans(orders[a][::-1])[i]
            copy = remote(
                grads[a].at[flip(s, tag + 1)],
                got_core[a].at[tag // 2],
                send_core.at[a, tag // 2],
                recv_core.at[a, tag // 2],
                (flip(s, 1), c),
            )
            copy.start()
            core_copies[a, tag] = copy
            load = pltpu.make_async_copy(
                grads[a].at[flip(s, tag)], acc[a].at[tag // 2], load_sem.at[a, tag // 2]
            )
            load.start()
            loads[a, tag] = load
    def fold(a, tag, k):
        rows = acc[a].shape[1]
        if k == 0:
            loads[a, tag].wait()
            core_copies[a, tag].wait_recv()
            add_into(acc[a].at[tag // 2], got_core[a].at[tag // 2], rows)
        else:
            copy, slot = late[a, k - 1, tag]
            copy.wait_recv()
            add_into(acc[a].at[tag // 2], got_late[a].at[slot], rows)

    base = 0
    for k in range(nb):
        count = 2 ** (nb - 1 - k)
        for i in range(count - 1, -1, -1):
            for a in range(n):
                bit = orders[a][k]
                kept = spans(orders[a][k + 1 :][::-1])[i]
                fold(a, kept + bit, k)
                copy = remote(
                    acc[a].at[(kept + bit) // 2],
                    got_late[a].at[base + i],
                    send_late.at[a, base + i],
                    recv_late.at[a, base + i],
                    (flip(s, bit), c),
                )
                copy.start()
                late[a, k, kept] = (copy, base + i)
        for i in range(count - 1, -1, -1):
            for a in range(n):
                fold(a, spans(orders[a][k + 1 :][::-1])[i], k)
        base += count
    writes = []
    for a in range(n):
        fold(a, 0, nb)
        write = pltpu.make_async_copy(acc[a].at[0], outs[a], out_sem.at[a])
        write.start()
        writes.append(write)
    for copy in core_copies.values():
        copy.wait_send()
    for copy, _ in late.values():
        copy.wait_send()
    for write in writes:
        write.wait()


def scatter_rows(grads, ns):
    half = ns // 2
    n = len(grads)
    any_spec = pl.BlockSpec(memory_space=pl.ANY)
    return pl.pallas_call(
        functools.partial(scatter_kernel, ns, n),
        out_shape=[jax.ShapeDtypeStruct(g.shape[1:], BF) for g in grads],
        in_specs=[any_spec] * n,
        out_specs=[any_spec] * n,
        scratch_shapes=[pltpu.VMEM((half,) + g.shape[1:], BF) for g in grads]
        + [pltpu.VMEM((half,) + g.shape[1:], BF) for g in grads]
        + [pltpu.VMEM((half - 1,) + g.shape[1:], BF) for g in grads]
        + [
            pltpu.SemaphoreType.DMA((n, half)),
            pltpu.SemaphoreType.DMA((n, half)),
            pltpu.SemaphoreType.DMA((n, half - 1)),
            pltpu.SemaphoreType.DMA((n, half - 1)),
            pltpu.SemaphoreType.DMA((n, half)),
            pltpu.SemaphoreType.DMA((n,)),
        ],
        compiler_params=pltpu.CompilerParams(
            collective_id=2, has_side_effects=True, vmem_limit_bytes=VMEM_BYTES
        ),
        cost_estimate=exchange_cost(95),
        name="scatter_rows",
    )(*grads)


class Parts:
    def __init__(self, parts, wide, send, recv, rooms, local_sem, s, c, rank):
        self.copies, self.keep, self.arrivals = [], [], []
        for a in range(len(parts)):
            for d in (2, 3, 1):
                copy = remote(
                    parts[a].at[flip(rank, d)],
                    wide[a].at[rank],
                    send.at[a, d],
                    recv.at[a, d],
                    (flip(s, d), c),
                )
                copy.start()
                self.copies.append(copy)
                block = wide[a].at[flip(rank, d)]
                self.arrivals.append(remote(block, block, send.at[a, d], recv.at[a, d], (s, c)))
            self.keep.append(Keep(parts[a].at[rank], wide[a].at[rank], rooms[a], local_sem.at[a]))

    def forward(self):
        for own in self.keep:
            own.forward()

    def finish(self):
        for arrival in self.arrivals:
            arrival.wait_recv()
        for own in self.keep:
            own.finish()
        for copy in self.copies:
            copy.wait_send()


class Share:
    def __init__(self, act, wide, send, recv, room, local_sem, s, c, rank):
        self.wide, self.send, self.recv, self.at, self.rank = wide, send, recv, (s, c), rank
        self.copies = []
        self.push(2, act)
        self.push(1, act)
        self.keep = Keep(act, wide.at[rank], room, local_sem)

    def push(self, d, src):
        s, c = self.at
        hop = 2 if d == 2 else 1
        copy = remote(
            src,
            self.wide.at[flip(self.rank, d - hop)],
            self.send.at[d],
            self.recv.at[d],
            (flip(s, hop), c),
        )
        copy.start()
        self.copies.append(copy)

    def arrived(self, d):
        block = self.wide.at[flip(self.rank, d)]
        remote(block, block, self.send.at[d], self.recv.at[d], self.at).wait_recv()

    def forward(self):
        self.keep.forward()
        self.arrived(2)
        self.push(3, self.wide.at[flip(self.rank, 2)])

    def finish(self):
        self.arrived(1)
        self.arrived(3)
        self.keep.finish()
        for copy in self.copies:
            copy.wait_send()


class Far:
    def __init__(self, weight, wide, send, recv, room, local_sem, s, c, ny):
        y = s // TP
        far = far_peers(s, c, ny)
        self.arrivals, self.copies = [], []
        for j in range(1, ny):
            copy = remote(weight, wide.at[y], send.at[j - 1], recv.at[j - 1], far[j - 1])
            copy.start()
            self.copies.append(copy)
            block = wide.at[(y + ny - j) % ny]
            self.arrivals.append(remote(block, block, send.at[j - 1], recv.at[j - 1], (s, c)))
        self.keep = Keep(weight, wide.at[y], room, local_sem)

    def forward(self):
        self.keep.forward()

    def finish(self):
        for arrival in self.arrivals:
            arrival.wait_recv()
        self.keep.finish()
        for copy in self.copies:
            copy.wait_send()


def far_peers(s, c, ny):
    return [((s // TP + j) % ny * TP + s % TP, c) for j in range(1, ny)]


class RowSum:
    def __init__(self, parts, out, part, core, far, send, recv, local_sem, s, c, rank):
        self.out, self.part, self.core, self.far, self.at = out, part, core, far, (s, c)
        self.send, self.recv, self.local_sem = send, recv, local_sem
        self.copies, self.loads = {}, {}
        for d in (2, 0):
            copy = remote(
                parts.at[flip(rank, d + 1)],
                core.at[d // 2],
                send.at[d // 2],
                recv.at[d // 2],
                (flip(s, 1), c),
            )
            copy.start()
            self.copies[d] = copy
            self.loads[d] = pltpu.make_async_copy(
                parts.at[flip(rank, d)], part.at[d // 2], local_sem.at[d // 2]
            )
            self.loads[d].start()

    def forward(self):
        s, c = self.at
        rows = self.part.shape[1]
        for d in (2, 0):
            self.loads[d].wait()
            self.copies[d].wait_recv()
            add_into(self.part.at[d // 2], self.core.at[d // 2], rows)
            if d == 2:
                copy = remote(
                    self.part.at[1], self.far, self.send.at[2], self.recv.at[2], (flip(s, 2), c)
                )
                copy.start()
                self.copies[3] = copy

    def finish(self):
        self.copies[3].wait_recv()
        add_into(self.part.at[0], self.far, self.part.shape[1])
        write = pltpu.make_async_copy(self.part.at[0], self.out, self.local_sem.at[2])
        write.start()
        for copy in self.copies.values():
            copy.wait_send()
        write.wait()


def quad_here():
    s, c = lax.axis_index("shard"), lax.axis_index("ctx")
    return s, c, s % TP


def first_kernel(ns, *refs):
    parts, small, passed, wide, all_small, passed_on = refs[:2], *refs[2:4], refs[4:6], *refs[6:8]
    send, recv, send_small, recv_small, local_sem = refs[8:13]
    rooms, small_room, passed_room = refs[13:15], *refs[15:]
    s, c, rank = quad_here()
    others = [((s + j) % ns, c) for j in range(1, ns)]
    greet(others)
    copies = []
    for j in range(1, ns):
        copy = remote(
            small, all_small.at[s], send_small.at[j - 1], recv_small.at[j - 1], others[j - 1]
        )
        copy.start()
        copies.append(copy)
    two = Parts(parts, wide, send, recv, rooms, local_sem, s, c, rank)
    own = Keep(small, all_small.at[s], small_room, local_sem.at[2])
    kept = Keep(passed, passed_on, passed_room, local_sem.at[3])
    own.forward()
    kept.forward()
    two.forward()
    for j in range(1, ns):
        block = all_small.at[(s + ns - j) % ns]
        remote(block, block, send_small.at[j - 1], recv_small.at[j - 1], (s, c)).wait_recv()
    two.finish()
    own.finish()
    kept.finish()
    for copy in copies:
        copy.wait_send()


def first_exchange(parts, small, passed, ns):
    any_spec = pl.BlockSpec(memory_space=pl.ANY)
    return pl.pallas_call(
        functools.partial(first_kernel, ns),
        out_shape=[jax.ShapeDtypeStruct(p.shape, BF) for p in parts]
        + [
            jax.ShapeDtypeStruct((ns,) + small.shape, BF),
            jax.ShapeDtypeStruct(passed.shape, BF),
        ],
        in_specs=[any_spec] * 4,
        out_specs=[any_spec] * 4,
        scratch_shapes=[
            pltpu.SemaphoreType.DMA((2, TP)),
            pltpu.SemaphoreType.DMA((2, TP)),
            pltpu.SemaphoreType.DMA((ns - 1,)),
            pltpu.SemaphoreType.DMA((ns - 1,)),
            pltpu.SemaphoreType.DMA((4, 2)),
        ]
        + [pltpu.VMEM(p.shape[1:], BF) for p in parts]
        + [pltpu.VMEM(x.shape, BF) for x in (small, passed)],
        compiler_params=pltpu.CompilerParams(collective_id=5, has_side_effects=True),
        cost_estimate=exchange_cost(25),
        name="first_exchange",
    )(*parts, small, passed)


def share_kernel(ny, weight, act, wide, wide_act, *refs):
    send_far, recv_far, send, recv, local_sem, room, act_room = refs
    s, c, rank = quad_here()
    greet([(flip(s, d), c) for d in (1, 2)] + far_peers(s, c, ny))
    far = Far(weight, wide, send_far, recv_far, room, local_sem.at[1], s, c, ny)
    rows = Share(act, wide_act, send, recv, act_room, local_sem.at[0], s, c, rank)
    far.forward()
    rows.forward()
    rows.finish()
    far.finish()


def share_scratch(weight, act, ny):
    return [
        pltpu.SemaphoreType.DMA((ny - 1,)),
        pltpu.SemaphoreType.DMA((ny - 1,)),
        pltpu.SemaphoreType.DMA((TP,)),
        pltpu.SemaphoreType.DMA((TP,)),
        pltpu.SemaphoreType.DMA((2, 2)),
        pltpu.VMEM(weight.shape, BF),
        pltpu.VMEM(act.shape, BF),
    ]


def share_rows(weight, act, ny):
    any_spec = pl.BlockSpec(memory_space=pl.ANY)
    return pl.pallas_call(
        functools.partial(share_kernel, ny),
        out_shape=[
            jax.ShapeDtypeStruct((ny,) + weight.shape, BF),
            jax.ShapeDtypeStruct((TP,) + act.shape, BF),
        ],
        in_specs=[any_spec] * 2,
        out_specs=[any_spec] * 2,
        scratch_shapes=share_scratch(weight, act, ny),
        compiler_params=pltpu.CompilerParams(
            collective_id=3, has_side_effects=True, vmem_limit_bytes=VMEM_BYTES
        ),
        cost_estimate=exchange_cost(60),
        name="share_rows",
    )(weight, act)


def sum_scratch(act):
    return [
        pltpu.VMEM((2,) + act, BF),
        pltpu.VMEM((2,) + act, BF),
        pltpu.VMEM(act, BF),
        pltpu.SemaphoreType.DMA((3,)),
        pltpu.SemaphoreType.DMA((3,)),
        pltpu.SemaphoreType.DMA((3,)),
    ]


def add_rows(target, other):
    def step(i, carry):
        rows = pl.ds(pl.multiple_of(i * 16, 16), 16)
        target[rows] = (target[rows].astype(F32) + other[rows].astype(F32)).astype(BF)
        return carry

    lax.fori_loop(0, target.shape[0] // 16, step, 0)


def middle_kernel(*refs):
    grad_hbm, fc_hbm, act_hbm, proj_hbm, in_hbm = refs[:5]
    sum_out, out_out, fc_out = refs[5:8]
    grad, w_fc, act, w_proj, act_in, out_part, grad_fc = refs[8:15]
    parts, core, far = refs[15:18]
    send, recv, load_sem, out_sem = refs[18:]
    s, c, rank = quad_here()
    loads = [
        pltpu.make_async_copy(src, dst, load_sem.at[i])
        for i, (src, dst) in enumerate(
            (
                (grad_hbm, grad),
                (fc_hbm, w_fc),
                (act_hbm, act),
                (proj_hbm, w_proj),
                (in_hbm, act_in),
            )
        )
    ]
    for load in loads:
        load.start()
    greet([(flip(s, d), c) for d in (1, 2)])
    rows = far.shape[0]
    loads[0].wait()
    loads[1].wait()

    def part(d):
        block = grad[pl.ds(pl.multiple_of(flip(rank, d) * rows, rows), rows), :]
        parts[d] = mm(block, w_fc[...], NT).astype(BF)

    copies = {}
    for d in (3, 1):
        part(d)
        copy = remote(
            parts.at[d], core.at[d // 2], send.at[d // 2], recv.at[d // 2], (flip(s, 1), c)
        )
        copy.start()
        copies[d] = copy
    part(2)
    copies[3].wait_recv()
    add_rows(parts.at[2], core.at[1])
    across = remote(parts.at[2], far, send.at[2], recv.at[2], (flip(s, 2), c))
    across.start()
    part(0)
    copies[1].wait_recv()
    add_rows(parts.at[0], core.at[0])
    loads[2].wait()
    loads[3].wait()
    step_rows = 256 if act.shape[0] % 256 == 0 else 128

    def out_step(i, carry):
        at = pl.ds(pl.multiple_of(i * step_rows, step_rows), step_rows)
        out_part[at, :] = mm(act[at, :], w_proj[...], NN).astype(BF)
        return carry

    lax.fori_loop(0, act.shape[0] // step_rows, out_step, 0)
    writes = [pltpu.make_async_copy(out_part, out_out, out_sem.at[0])]
    writes[0].start()
    loads[4].wait()
    width = act_in.shape[1]

    def fc_step(i, carry):
        at = pl.ds(pl.multiple_of(i * 256, 256), 256)
        grad_fc[at, :] = mm(act_in[:, at], grad[...], TN).astype(BF)
        return carry

    lax.fori_loop(0, width // 256, fc_step, 0)
    if width % 256:
        at = pl.ds(width // 256 * 256, width % 256)
        grad_fc[at, :] = mm(act_in[:, at], grad[...], TN).astype(BF)
    writes.append(pltpu.make_async_copy(grad_fc, fc_out, out_sem.at[1]))
    writes[1].start()
    across.wait_recv()
    add_rows(parts.at[0], far)
    writes.append(pltpu.make_async_copy(parts.at[0], sum_out, out_sem.at[2]))
    writes[2].start()
    for copy in copies.values():
        copy.wait_send()
    across.wait_send()
    for write in writes:
        write.wait()


def middle_rows(grad, w_fc, act, w_proj, act_in):
    any_spec = pl.BlockSpec(memory_space=pl.ANY)
    rows = grad.shape[0] // TP
    width = act_in.shape[1]
    return pl.pallas_call(
        middle_kernel,
        out_shape=[
            jax.ShapeDtypeStruct((rows, width), BF),
            jax.ShapeDtypeStruct((TP * rows, w_proj.shape[1]), BF),
            jax.ShapeDtypeStruct((width, grad.shape[1]), BF),
        ],
        in_specs=[any_spec] * 5,
        out_specs=[any_spec] * 3,
        scratch_shapes=[pltpu.VMEM(x.shape, BF) for x in (grad, w_fc, act, w_proj, act_in)]
        + [
            pltpu.VMEM((TP * rows, w_proj.shape[1]), BF),
            pltpu.VMEM((width, grad.shape[1]), BF),
            pltpu.VMEM((TP, rows, width), BF),
            pltpu.VMEM((2, rows, width), BF),
            pltpu.VMEM((rows, width), BF),
            pltpu.SemaphoreType.DMA((3,)),
            pltpu.SemaphoreType.DMA((3,)),
            pltpu.SemaphoreType.DMA((5,)),
            pltpu.SemaphoreType.DMA((3,)),
        ],
        compiler_params=pltpu.CompilerParams(
            collective_id=4, has_side_effects=True, vmem_limit_bytes=VMEM_BYTES
        ),
        cost_estimate=exchange_cost(50),
        name="middle_rows",
    )(grad, w_fc, act, w_proj, act_in)


def last_kernel(*refs):
    parts, wide = refs[:2], refs[3:5]
    send, recv, local_sem = refs[5:8]
    s, c, rank = quad_here()
    greet([(flip(s, d), c) for d in (1, 2, 3)])
    two = Parts(parts, wide, send, recv, refs[8:], local_sem, s, c, rank)
    two.forward()
    two.finish()


def last_exchange(parts, ready):
    any_spec = pl.BlockSpec(memory_space=pl.ANY)
    return pl.pallas_call(
        last_kernel,
        out_shape=[jax.ShapeDtypeStruct(p.shape, BF) for p in parts],
        in_specs=[any_spec] * 3,
        out_specs=[any_spec] * 2,
        scratch_shapes=[
            pltpu.SemaphoreType.DMA((2, TP)),
            pltpu.SemaphoreType.DMA((2, TP)),
            pltpu.SemaphoreType.DMA((2, 2)),
        ]
        + [pltpu.VMEM(p.shape[1:], BF) for p in parts],
        compiler_params=pltpu.CompilerParams(collective_id=6, has_side_effects=True),
        cost_estimate=exchange_cost(20),
        name="last_exchange",
    )(*parts, ready)


NN = (((1,), (0,)), ((), ()))
NT = (((1,), (1,)), ((), ()))
TN = (((0,), (0,)), ((), ()))


def mm(left, right, dims):
    return lax.dot_general(left, right, dims, preferred_element_type=F32)


def halves(rows):
    lane = lax.broadcasted_iota(jnp.int32, (rows, 2 * HD), 1)
    return lane < HD


def one_of(values, low, head):
    return jnp.where(low if head == 0 else jnp.logical_not(low), values, jnp.zeros_like(values))


def for_pairs(width, body, between):
    pairs = width // (2 * HD)

    def step(i, carry):
        body(pl.ds(pl.multiple_of(i * 2 * HD, 2 * HD), 2 * HD), 2 * i, 2)
        return carry

    start = 0
    for n, extra in enumerate(between):
        stop = pairs * (n + 1) // (len(between) + 1)
        lax.fori_loop(start, stop, step, 0)
        extra()
        start = stop
    lax.fori_loop(start, pairs, step, 0)
    if width % (2 * HD):
        body(pl.ds(pairs * 2 * HD, HD), 2 * pairs, 1)


def attend_kernel(ny, *refs):
    q_ref, k_ref, v_ref, bias_ref, weight, act = refs[:6]
    o_ref, lse_ref, wide, wide_act, token = refs[6:11]
    send_far, recv_far, send_act, recv_act, local_sem, room, act_room = refs[11:]
    token[0] = jnp.int32(0)
    width = q_ref.shape[1]
    low = halves(k_ref.shape[0])
    s, c, rank = quad_here()
    greet([(flip(s, d), c) for d in (1, 2)] + far_peers(s, c, ny))
    far = Far(weight, wide, send_far, recv_far, room, local_sem.at[1], s, c, ny)
    rows = Share(act, wide_act, send_act, recv_act, act_room, local_sem.at[0], s, c, rank)

    def body(cols, first, count):
        q = q_ref[:, cols]
        k = k_ref[:, cols]
        v = v_ref[:, cols]
        total = None
        for head in range(count):
            k_h = one_of(k, low, head) if count == 2 else k
            v_h = one_of(v, low, head) if count == 2 else v
            scores = mm(q, k_h, NT) + bias_ref[...]
            peak = jnp.max(scores, axis=1, keepdims=True)
            weights = jnp.exp(scores - peak)
            norm = jnp.sum(weights, axis=1, keepdims=True)
            part = mm(weights.astype(BF), v_h, NN) / norm
            total = part if total is None else total + part
            lse_ref[first + head] = peak + jnp.log(norm)
        o_ref[:, cols] = total.astype(BF)

    for_pairs(width, body, [far.forward, lambda: None, lambda: None])
    rows.forward()
    rows.finish()
    far.finish()


def attend_forward(q, k, v, bias, weight, act, ny):
    heads = q.shape[1] // HD
    vmem = pl.BlockSpec(memory_space=pltpu.VMEM)
    any_spec = pl.BlockSpec(memory_space=pl.ANY)
    return pl.pallas_call(
        functools.partial(attend_kernel, ny),
        out_shape=[
            jax.ShapeDtypeStruct(q.shape, BF),
            jax.ShapeDtypeStruct((heads, q.shape[0], 1), F32),
            jax.ShapeDtypeStruct((ny,) + weight.shape, BF),
            jax.ShapeDtypeStruct((TP,) + act.shape, BF),
            jax.ShapeDtypeStruct((1,), jnp.int32),
        ],
        in_specs=[vmem] * 4 + [any_spec] * 2,
        out_specs=[vmem] * 2 + [any_spec] * 2 + [pl.BlockSpec(memory_space=pltpu.SMEM)],
        scratch_shapes=share_scratch(weight, act, ny),
        compiler_params=pltpu.CompilerParams(
            collective_id=7, has_side_effects=True, vmem_limit_bytes=VMEM_BYTES
        ),
        cost_estimate=exchange_cost(60),
        name="attend_forward",
    )(q, k, v, bias, weight, act)


def attend_back_kernel(*refs):
    q_ref, k_ref, v_ref, g_ref, lse_ref, bias_ref, _, parts = refs[:8]
    dq_ref, dk_ref, dv_ref, out = refs[8:12]
    width = q_ref.shape[1]
    low_q = halves(q_ref.shape[0])
    low_k = halves(k_ref.shape[0])
    scale = 1.0 / math.sqrt(HD)
    s, c, rank = quad_here()
    greet([(flip(s, d), c) for d in (1, 2)])
    rows = RowSum(parts, out, *refs[12:], s, c, rank)

    def body(cols, first, count):
        q = q_ref[:, cols]
        k = k_ref[:, cols]
        v = v_ref[:, cols]
        g = g_ref[:, cols]
        dq = dk = dv = None
        for head in range(count):
            if count == 2:
                q_h, g_h = one_of(q, low_q, head), one_of(g, low_q, head)
                k_h = one_of(k, low_k, head)
            else:
                q_h, g_h, k_h = q, g, k
            scores = mm(k, q_h, NT) + bias_ref[...]
            probs = jnp.exp(scores - lse_ref[first + head])
            grad = mm(v, g_h, NT)
            both = probs * grad
            centre = jnp.sum(both, axis=0, keepdims=True)
            ds = (both - probs * centre).astype(BF)
            dq_h = mm(ds, k_h, TN)
            dk_h = mm(ds, q_h, NN)
            dv_h = mm(probs.astype(BF), g_h, NN)
            dq = dq_h if dq is None else dq + dq_h
            dk = dk_h if dk is None else dk + dk_h
            dv = dv_h if dv is None else dv + dv_h
        dq_ref[:, cols] = (dq * scale).astype(BF)
        dk_ref[:, cols] = dk.astype(BF)
        dv_ref[:, cols] = dv.astype(BF)

    for_pairs(width, body, [rows.forward, lambda: None, lambda: None])
    rows.finish()


def attend_backward(q, k, v, g, lse, bias, ready, parts):
    vmem = pl.BlockSpec(memory_space=pltpu.VMEM)
    any_spec = pl.BlockSpec(memory_space=pl.ANY)
    act = parts.shape[1:]
    return pl.pallas_call(
        attend_back_kernel,
        out_shape=[jax.ShapeDtypeStruct(x.shape, BF) for x in (q, k, v)]
        + [jax.ShapeDtypeStruct(act, BF)],
        in_specs=[vmem] * 6 + [any_spec] * 2,
        out_specs=[vmem] * 3 + [any_spec],
        scratch_shapes=sum_scratch(act),
        compiler_params=pltpu.CompilerParams(
            collective_id=8, has_side_effects=True, vmem_limit_bytes=VMEM_BYTES
        ),
        cost_estimate=exchange_cost(47),
        name="attend_backward",
    )(q, k, v, g, lse, bias, ready, parts)


def normed(values):
    mean = jnp.mean(values, axis=-1, keepdims=True)
    centred = values - mean
    spread = jnp.mean(centred * centred, axis=-1, keepdims=True)
    inverse = lax.rsqrt(spread + NORM_EPS)
    return centred * inverse, inverse


def norm_back(u, unit, inverse, gain):
    gu = gain * u
    grad = inverse * (
        gu - jnp.mean(gu, axis=-1, keepdims=True) - unit * jnp.mean(gu * unit, axis=-1, keepdims=True)
    )
    return grad, jnp.sum(u * unit, axis=0), jnp.sum(u, axis=0)


def adamw(master, first, second, gradient, rate, decay):
    first_new = BETA_ONE * first + (1.0 - BETA_ONE) * gradient
    second_new = BETA_TWO * second + (1.0 - BETA_TWO) * gradient * gradient
    fix_one = 1.0 - BETA_ONE**STEP
    fix_two = 1.0 - BETA_TWO**STEP
    update = first_new / fix_one / (jnp.sqrt(second_new / fix_two) + ADAM_EPS)
    master_new = master - rate * (update + decay * master)
    return (master_new, first_new, second_new, master_new.astype(BF))


def cuts(start, stop, width):
    found = []
    while start < stop:
        block, low = divmod(start, width)
        high = min(width, low + stop - start)
        found.append((block, low, high))
        start += high - low
    return found


def after(first, later):
    return lax.optimization_barrier((first, later))[1]


def behind(token, value):
    return jnp.where(token[0] == 0, value, jnp.zeros_like(value))


def local(
    tokens,
    cotangent,
    master_qkv,
    master_out,
    master_fc,
    master_proj,
    master_small,
    first_qkv,
    first_out,
    first_fc,
    first_proj,
    first_small,
    second_qkv,
    second_out,
    second_fc,
    second_proj,
    second_small,
):
    ns, nc = lax.axis_size("shard"), lax.axis_size("ctx")
    s, c = lax.axis_index("shard"), lax.axis_index("ctx")
    ny = ns // TP
    rank = s % TP
    rows = tokens.shape[0]
    prompt_rows = PROMPT // nc
    kr = D // ns
    hs = FF // ns // TP
    hq = ns * hs
    hc = hq // nc
    oc = D // nc
    pack = 8 if kr % 8 == 0 else 4
    packed = (kr // pack, pack, D)
    act_pack = (rows // 8, 8, D)
    far_groups = [[y * TP + r for y in range(ny)] for r in range(TP)]

    qc = master_qkv.shape[1]
    attn_block = jnp.concatenate([master_qkv.astype(BF), master_out.astype(BF)], axis=1)
    attn_z = lax.all_gather(attn_block, "ctx", axis=0)
    fc_parts = master_fc.astype(BF).reshape(kr, ns // nc, TP, hs).transpose(2, 0, 1, 3)
    proj_parts = master_proj.astype(BF).reshape(TP, hs, D // nc)
    fc_quad, proj_quad, small_all, prompt_own = first_exchange(
        [fc_parts.reshape(TP, kr, hc), proj_parts],
        master_small.astype(BF),
        tokens[:prompt_rows],
        ns,
    )
    small = small_all.transpose(1, 0, 2).reshape(master_small.shape[0], D).astype(F32)
    prompt_tokens = lax.all_gather(prompt_own, "ctx", axis=0, tiled=True)
    fc_z = lax.all_gather(after(attn_z, fc_quad), "ctx", axis=0)
    proj_z = lax.all_gather(after(attn_z, proj_quad), "ctx", axis=0)

    qkv_rows = [
        jnp.concatenate(
            [attn_z[b, :, low:high] for b, low, high in cuts(i * D, (i + 1) * D, qc)], axis=1
        )
        for i in range(3)
    ]
    out_rows = jnp.concatenate([attn_z[b, :, qc:] for b in range(nc)], axis=1)
    gathered = gather_rows([w.reshape(packed) for w in qkv_rows + [out_rows]], ns)
    w_q, w_k, w_v, w_o = [w.reshape(D, D) for w in gathered[:4]]
    fc_z = behind(gathered[4], fc_z).reshape(nc, TP * kr, hc)
    fc_rows = jnp.concatenate([fc_z[b] for b in range(nc)], axis=1)

    own = tokens.astype(F32)
    unit_one, inverse_one = normed(own)
    all_rows = jnp.concatenate([prompt_tokens, tokens[prompt_rows:]], axis=0).astype(F32)
    unit_all = normed(all_rows)[0]
    act_all = (unit_all * small[0] + small[1]).astype(BF)
    act_one = jnp.concatenate(
        [lax.dynamic_slice_in_dim(act_all, c * prompt_rows, prompt_rows), act_all[PROMPT:]], axis=0
    )
    scale = 1.0 / math.sqrt(HD)
    q = (mm(act_one, w_q, NN) + small[4]).astype(BF) * BF(scale)
    k = mm(act_all, w_k, NN).astype(BF)
    v = (mm(act_all, w_v, NN) + small[5]).astype(BF)
    places = jnp.arange(rows, dtype=jnp.int32)
    in_prompt = places < prompt_rows
    later = places - prompt_rows
    pos_query = jnp.where(in_prompt, c * prompt_rows + places, PROMPT + later % BLK)
    seq_query = jnp.where(in_prompt, -1, later // BLK)
    cont_keys = jnp.arange(rows - prompt_rows, dtype=jnp.int32)
    pos_key = jnp.concatenate([jnp.arange(PROMPT, dtype=jnp.int32), PROMPT + cont_keys % BLK])
    seq_key = jnp.concatenate([jnp.full((PROMPT,), -1, jnp.int32), cont_keys // BLK])
    allowed = (pos_key[None, :] <= pos_query[:, None]) & (
        (seq_key[None, :] == -1) | (seq_key[None, :] == seq_query[:, None])
    )
    bias = jnp.where(allowed, 0.0, MASKED).astype(F32)
    attended, log_totals, w_fc, cot_wide, token = attend_forward(
        q, k, v, bias, fc_rows.reshape(TP * packed[0], pack, hq), cotangent.reshape(act_pack), ny
    )
    middle = own + mm(attended, w_o, NN) + small[6]
    unit_two, inverse_two = normed(middle)
    act_two = (unit_two * small[2] + small[3]).astype(BF)

    proj_z = behind(token, proj_z).reshape(nc, TP * hs, oc)
    proj_rows = jnp.concatenate([proj_z[b] for b in range(nc)], axis=1)
    pack_hs = 8 if hs % 8 == 0 else 4
    w_proj, act_wide = share_rows(
        proj_rows.reshape(TP * hs // pack_hs, pack_hs, D), act_two.reshape(act_pack), ny
    )
    w_fc = w_fc.reshape(D, hq)
    w_proj = w_proj.reshape(hq, D)
    act_wide = act_wide.reshape(TP * rows, D)
    cot_wide = cot_wide.reshape(TP * rows, D)
    fc_bias = lax.dynamic_index_in_dim(
        small[7 : 7 + FF // D].reshape(ns, TP, hs), rank, axis=1, keepdims=False
    ).reshape(hq)
    hidden = mm(act_wide, w_fc, NN) + fc_bias
    cube = 0.7978845608028654 * (hidden + 0.044715 * hidden * hidden * hidden)
    bent = jnp.tanh(cube)
    act_three = (0.5 * hidden * (1.0 + bent)).astype(BF)
    slope = 0.5 * (1.0 + bent) + 0.5 * hidden * (1.0 - bent * bent) * 0.7978845608028654 * (
        1.0 + 3.0 * 0.044715 * hidden * hidden
    )
    grad_hidden = (mm(cot_wide, w_proj, NT) * slope).astype(BF)
    grad_proj = mm(act_three, cot_wide, TN).astype(BF)
    proj_far = lax.psum_scatter(
        grad_proj, "shard", scatter_dimension=0, tiled=True, axis_index_groups=far_groups
    )
    mid_sum, out_part, grad_fc = middle_rows(grad_hidden, w_fc, act_three, w_proj, act_wide)
    grad_fc_bias = jnp.sum(grad_hidden, axis=0, dtype=F32)
    fc_far = lax.psum_scatter(
        grad_fc, "shard", scatter_dimension=0, tiled=True, axis_index_groups=far_groups
    )
    proj_far = proj_far.reshape(TP * hs, nc, D // nc).transpose(1, 0, 2)
    proj_near = lax.psum_scatter(proj_far, "ctx", scatter_dimension=0)
    fc_far = fc_far.reshape(TP * kr, nc, hc).transpose(1, 0, 2)
    fc_near = lax.psum_scatter(fc_far, "ctx", scatter_dimension=0)

    grad_output = cotangent.astype(F32)
    grad_norm, gain_two, shift_two = norm_back(
        mid_sum.astype(F32), unit_two, inverse_two, small[2]
    )
    grad_middle = grad_output + grad_norm
    grad_branch = grad_middle.astype(BF)
    grad_wo = mm(attended, grad_branch, TN).astype(BF)
    grad_attended = mm(grad_branch, w_o, NT).astype(BF)
    grad_q, grad_k, grad_v, out_sum = attend_backward(
        q, k, v, grad_attended, log_totals.transpose(0, 2, 1), bias.T, proj_far,
        out_part.reshape((TP,) + act_pack),
    )
    output = middle + out_sum.reshape(rows, D).astype(F32) + small[small.shape[0] - 1]
    key_part = mm(grad_k, w_k, NT) + mm(grad_v, w_v, NT)
    prompt_sum = lax.psum_scatter(
        key_part[:PROMPT].astype(BF), "ctx", scatter_dimension=0, tiled=True
    )
    query_part = mm(grad_q, w_q, NT)
    grad_wq = mm(act_one, grad_q, TN).astype(BF)
    grad_wk = mm(act_all, grad_k, TN).astype(BF)
    grad_wv = mm(act_all, grad_v, TN).astype(BF)

    hidden_grads = lax.dynamic_update_index_in_dim(
        jnp.zeros((ns, TP, hs), F32), grad_fc_bias.reshape(ns, 1, hs), rank, axis=1
    )
    small_grads = jnp.concatenate(
        [
            jnp.stack(
                [
                    jnp.sum(key_part * unit_all, axis=0) + jnp.sum(query_part * unit_one, axis=0),
                    jnp.sum(key_part, axis=0) + jnp.sum(query_part, axis=0),
                    gain_two,
                    shift_two,
                    jnp.sum(grad_q, axis=0, dtype=F32),
                    jnp.sum(grad_v, axis=0, dtype=F32),
                    jnp.sum(grad_branch, axis=0, dtype=F32),
                ]
            ),
            hidden_grads.reshape(FF // D, D),
            jnp.sum(grad_output, axis=0)[None],
        ],
        axis=0,
    )
    n_small = small_grads.shape[0]
    small_parts = small_grads.reshape(n_small, ns, kr).transpose(1, 0, 2).reshape(ns, n_small * kr)
    small_parts = jnp.pad(small_parts, ((0, 0), (0, 8 * D - n_small * kr)))
    back_q, back_k, back_v, back_o, back_small = scatter_rows(
        [g.reshape((ns,) + packed) for g in (grad_wq, grad_wk, grad_wv, grad_wo)]
        + [small_parts.astype(BF).reshape(ns, 1, 8, D)],
        ns,
    )
    fc_back, proj_back = last_exchange(
        [fc_near.reshape(TP, kr, hc), proj_near.reshape(TP, hs, D // nc)], back_small
    )
    qkv_back = [b.reshape(kr, D) for b in (back_q, back_k, back_v)]
    back_o = back_o.reshape(kr, D)
    attn_back = jnp.stack(
        [
            jnp.concatenate(
                [qkv_back[i][:, low:high] for i, low, high in cuts(b * qc, (b + 1) * qc, D)]
                + [back_o[:, b * oc : (b + 1) * oc]],
                axis=1,
            )
            for b in range(nc)
        ]
    )
    wide_rows = attn_back.shape[2]
    small_back = back_small.reshape(8 * D)[: 8 * wide_rows].reshape(1, 8, wide_rows)
    grad_attn = lax.psum_scatter(
        jnp.concatenate([attn_back, jnp.broadcast_to(small_back, (nc, 8, wide_rows))], axis=1),
        "ctx",
        scatter_dimension=0,
    )
    small_own = grad_attn[kr:].reshape(-1)[: n_small * kr].reshape(n_small, kr).astype(F32)
    grad_act = query_part + jnp.concatenate(
        [prompt_sum.astype(F32), key_part[PROMPT:]], axis=0
    )
    grad_norm, _, _ = norm_back(grad_act, unit_one, inverse_one, small[0])
    grad_input = grad_middle + grad_norm

    gradients = (
        grad_attn[:kr, :qc].astype(F32),
        grad_attn[:kr, qc:].astype(F32),
        fc_back.reshape(TP, kr, ns // nc, hs).transpose(1, 2, 0, 3).reshape(kr, FF // nc).astype(F32),
        proj_back.reshape(TP * hs, D // nc).astype(F32),
        small_own,
    )
    masters = (master_qkv, master_out, master_fc, master_proj, master_small)
    firsts = (first_qkv, first_out, first_fc, first_proj, first_small)
    seconds = (second_qkv, second_out, second_fc, second_proj, second_small)
    rates = (D ** (-0.5), max(D // 256, 1) ** (-0.5), D ** (-0.5), FF ** (-0.5), SMALL_RATE)
    decays = (WEIGHT_DECAY, WEIGHT_DECAY, WEIGHT_DECAY, WEIGHT_DECAY, 0.0)
    results = [
        adamw(masters[i], firsts[i], seconds[i], gradients[i], rates[i], decays[i]) for i in range(5)
    ]
    return (output.astype(BF), grad_input) + tuple(results[i][j] for j in range(4) for i in range(5))


def solution(mesh):
    row_spec = P(("shard", "ctx"), None)
    weight_specs = (P("shard", "ctx"),) * 4 + (P(None, "shard"),)
    return jax.shard_map(
        local,
        mesh=mesh,
        in_specs=(row_spec, row_spec) + weight_specs * 3,
        out_specs=(row_spec, row_spec) + weight_specs * 4,
        check_vma=False,
    )
```

```python
import functools
import math

import jax
import jax.numpy as jnp
from jax import lax
from jax.experimental import pallas as pl
from jax.experimental.pallas import tpu as pltpu
from jax.sharding import PartitionSpec as P

D = 1600
HD = 64
FF = 6400
BLK = 128
PROMPT = 1024
STEP = 10
TP = 4

NORM_EPS = 1e-05
BETA_ONE = 0.9
BETA_TWO = 0.999
ADAM_EPS = 1e-08
WEIGHT_DECAY = 0.1
SMALL_RATE = 0.2
MASKED = -1e30
MESH = pl.DeviceIdType.MESH
BF = jnp.bfloat16
F32 = jnp.float32
VMEM_BYTES = 60 * 1024 * 1024


def flip(index, mask):
    bit = 1
    while bit <= mask:
        if mask & bit:
            index = index + bit - 2 * bit * ((index // bit) % 2)
        bit *= 2
    return index


def spans(bits):
    tags = [0]
    for bit in bits:
        tags = tags + [t + bit for t in tags]
    return tags


def exchange_cost(us):
    return pl.CostEstimate(flops=0, bytes_accessed=us * 3_000_000, transcendentals=0)


def greet(peers):
    barrier = pltpu.get_barrier_semaphore()
    for peer in peers:
        pl.semaphore_signal(barrier, inc=1, device_id=peer, device_id_type=MESH)
    pl.semaphore_wait(barrier, len(peers))


def remote(src, dst, send, recv, peer):
    return pltpu.make_async_remote_copy(
        src_ref=src, dst_ref=dst, send_sem=send, recv_sem=recv, device_id=peer, device_id_type=MESH
    )


class Keep:
    def __init__(self, src, dst, room, sems):
        self.load = pltpu.make_async_copy(src, room, sems.at[0])
        self.store = pltpu.make_async_copy(room, dst, sems.at[1])
        self.load.start()

    def forward(self):
        self.load.wait()
        self.store.start()

    def finish(self):
        self.store.wait()


def add_into(target, other, rows):
    def step(i, carry):
        target[i] = (target[i].astype(F32) + other[i].astype(F32)).astype(BF)
        return carry

    lax.fori_loop(0, rows, step, 0)


def gather_kernel(ns, *refs):
    srcs, dsts, token = refs[:4], refs[4:8], refs[8]
    send, recv, local_sem = refs[9:12]
    rooms = refs[12:]
    token[0] = jnp.int32(0)
    s, c = lax.axis_index("shard"), lax.axis_index("ctx")
    bits = [1 << k for k in range(1, ns.bit_length() - 1)]
    greet([(flip(s, b), c) for b in [1] + bits])
    orders = [bits, bits, bits[::-1], bits[::-1]]

    def push(a, tag, bit):
        block = dsts[a].at[flip(s, tag)]
        got = tag + bit
        copy = remote(
            srcs[a] if tag == 0 else block, block, send.at[a, got], recv.at[a, got], (flip(s, bit), c)
        )
        copy.start()
        return copy

    def arrived(a, tag):
        block = dsts[a].at[flip(s, tag)]
        remote(block, block, send.at[a, tag], recv.at[a, tag], (s, c)).wait_recv()

    copies = []
    for k in range(len(bits)):
        for a in range(4):
            copies.append(push(a, 0, orders[a][k]))
    for a in range(4):
        copies.append(push(a, 0, 1))
    keep = [Keep(srcs[a], dsts[a].at[s], rooms[a], local_sem.at[a]) for a in range(4)]
    for own in keep:
        own.forward()
    for i in range(1, len(spans(bits))):
        for a in range(4):
            tag = spans(orders[a])[i]
            arrived(a, tag)
            last = max(k for k, b in enumerate(orders[a]) if tag & b)
            for b in orders[a][last + 1 :]:
                copies.append(push(a, tag, b))
            copies.append(push(a, tag, 1))
    for own in keep:
        own.finish()
    for a in range(4):
        for tag in spans(bits):
            arrived(a, tag + 1)
    for copy in copies:
        copy.wait_send()


def gather_rows(blocks, ns):
    any_spec = pl.BlockSpec(memory_space=pl.ANY)
    return pl.pallas_call(
        functools.partial(gather_kernel, ns),
        out_shape=[jax.ShapeDtypeStruct((ns,) + b.shape, b.dtype) for b in blocks]
        + [jax.ShapeDtypeStruct((1,), jnp.int32)],
        in_specs=[any_spec] * 4,
        out_specs=[any_spec] * 4 + [pl.BlockSpec(memory_space=pltpu.SMEM)],
        scratch_shapes=[
            pltpu.SemaphoreType.DMA((4, ns)),
            pltpu.SemaphoreType.DMA((4, ns)),
            pltpu.SemaphoreType.DMA((4, 2)),
        ]
        + [pltpu.VMEM(b.shape, BF) for b in blocks],
        compiler_params=pltpu.CompilerParams(collective_id=1, has_side_effects=True),
        cost_estimate=exchange_cost(95),
        name="gather_rows",
    )(*blocks)


def scatter_kernel(ns, n, *refs):
    grads, outs = refs[:n], refs[n : 2 * n]
    refs = refs[2 * n :]
    acc, got_core, got_late = refs[:n], refs[n : 2 * n], refs[2 * n : 3 * n]
    send_core, recv_core, send_late, recv_late, load_sem, out_sem = refs[3 * n :]
    s, c = lax.axis_index("shard"), lax.axis_index("ctx")
    bits = [1 << k for k in range(1, ns.bit_length() - 1)]
    nb = len(bits)
    greet([(flip(s, b), c) for b in [1] + bits])
    orders = [bits if a % 2 == 0 else bits[::-1] for a in range(n)]
    core_copies, loads, late = {}, {}, {}
    for i in range(ns // 2 - 1, -1, -1):
        for a in range(n):
            tag = spans(orders[a][::-1])[i]
            copy = remote(
                grads[a].at[flip(s, tag + 1)],
                got_core[a].at[tag // 2],
                send_core.at[a, tag // 2],
                recv_core.at[a, tag // 2],
                (flip(s, 1), c),
            )
            copy.start()
            core_copies[a, tag] = copy
            load = pltpu.make_async_copy(
                grads[a].at[flip(s, tag)], acc[a].at[tag // 2], load_sem.at[a, tag // 2]
            )
            load.start()
            loads[a, tag] = load
    def fold(a, tag, k):
        rows = acc[a].shape[1]
        if k == 0:
            loads[a, tag].wait()
            core_copies[a, tag].wait_recv()
            add_into(acc[a].at[tag // 2], got_core[a].at[tag // 2], rows)
        else:
            copy, slot = late[a, k - 1, tag]
            copy.wait_recv()
            add_into(acc[a].at[tag // 2], got_late[a].at[slot], rows)

    base = 0
    for k in range(nb):
        count = 2 ** (nb - 1 - k)
        for i in range(count - 1, -1, -1):
            for a in range(n):
                bit = orders[a][k]
                kept = spans(orders[a][k + 1 :][::-1])[i]
                fold(a, kept + bit, k)
                copy = remote(
                    acc[a].at[(kept + bit) // 2],
                    got_late[a].at[base + i],
                    send_late.at[a, base + i],
                    recv_late.at[a, base + i],
                    (flip(s, bit), c),
                )
                copy.start()
                late[a, k, kept] = (copy, base + i)
        for i in range(count - 1, -1, -1):
            for a in range(n):
                fold(a, spans(orders[a][k + 1 :][::-1])[i], k)
        base += count
    writes = []
    for a in range(n):
        fold(a, 0, nb)
        write = pltpu.make_async_copy(acc[a].at[0], outs[a], out_sem.at[a])
        write.start()
        writes.append(write)
    for copy in core_copies.values():
        copy.wait_send()
    for copy, _ in late.values():
        copy.wait_send()
    for write in writes:
        write.wait()


def scatter_rows(grads, ns):
    half = ns // 2
    n = len(grads)
    any_spec = pl.BlockSpec(memory_space=pl.ANY)
    return pl.pallas_call(
        functools.partial(scatter_kernel, ns, n),
        out_shape=[jax.ShapeDtypeStruct(g.shape[1:], BF) for g in grads],
        in_specs=[any_spec] * n,
        out_specs=[any_spec] * n,
        scratch_shapes=[pltpu.VMEM((half,) + g.shape[1:], BF) for g in grads]
        + [pltpu.VMEM((half,) + g.shape[1:], BF) for g in grads]
        + [pltpu.VMEM((half - 1,) + g.shape[1:], BF) for g in grads]
        + [
            pltpu.SemaphoreType.DMA((n, half)),
            pltpu.SemaphoreType.DMA((n, half)),
            pltpu.SemaphoreType.DMA((n, half - 1)),
            pltpu.SemaphoreType.DMA((n, half - 1)),
            pltpu.SemaphoreType.DMA((n, half)),
            pltpu.SemaphoreType.DMA((n,)),
        ],
        compiler_params=pltpu.CompilerParams(
            collective_id=2, has_side_effects=True, vmem_limit_bytes=VMEM_BYTES
        ),
        cost_estimate=exchange_cost(95),
        name="scatter_rows",
    )(*grads)


class Parts:
    def __init__(self, parts, wide, send, recv, rooms, local_sem, s, c, rank):
        self.copies, self.keep, self.arrivals = [], [], []
        for a in range(len(parts)):
            for d in (2, 3, 1):
                copy = remote(
                    parts[a].at[flip(rank, d)],
                    wide[a].at[rank],
                    send.at[a, d],
                    recv.at[a, d],
                    (flip(s, d), c),
                )
                copy.start()
                self.copies.append(copy)
                block = wide[a].at[flip(rank, d)]
                self.arrivals.append(remote(block, block, send.at[a, d], recv.at[a, d], (s, c)))
            self.keep.append(Keep(parts[a].at[rank], wide[a].at[rank], rooms[a], local_sem.at[a]))

    def forward(self):
        for own in self.keep:
            own.forward()

    def finish(self):
        for arrival in self.arrivals:
            arrival.wait_recv()
        for own in self.keep:
            own.finish()
        for copy in self.copies:
            copy.wait_send()


class Share:
    def __init__(self, act, wide, send, recv, room, local_sem, s, c, rank):
        self.wide, self.send, self.recv, self.at, self.rank = wide, send, recv, (s, c), rank
        self.copies = []
        self.push(2, act)
        self.push(1, act)
        self.keep = Keep(act, wide.at[rank], room, local_sem)

    def push(self, d, src):
        s, c = self.at
        hop = 2 if d == 2 else 1
        copy = remote(
            src,
            self.wide.at[flip(self.rank, d - hop)],
            self.send.at[d],
            self.recv.at[d],
            (flip(s, hop), c),
        )
        copy.start()
        self.copies.append(copy)

    def arrived(self, d):
        block = self.wide.at[flip(self.rank, d)]
        remote(block, block, self.send.at[d], self.recv.at[d], self.at).wait_recv()

    def forward(self):
        self.keep.forward()
        self.arrived(2)
        self.push(3, self.wide.at[flip(self.rank, 2)])

    def finish(self):
        self.arrived(1)
        self.arrived(3)
        self.keep.finish()
        for copy in self.copies:
            copy.wait_send()


class Far:
    def __init__(self, weight, wide, send, recv, room, local_sem, s, c, ny):
        y = s // TP
        far = far_peers(s, c, ny)
        self.arrivals, self.copies = [], []
        for j in range(1, ny):
            copy = remote(weight, wide.at[y], send.at[j - 1], recv.at[j - 1], far[j - 1])
            copy.start()
            self.copies.append(copy)
            block = wide.at[(y + ny - j) % ny]
            self.arrivals.append(remote(block, block, send.at[j - 1], recv.at[j - 1], (s, c)))
        self.keep = Keep(weight, wide.at[y], room, local_sem)

    def forward(self):
        self.keep.forward()

    def finish(self):
        for arrival in self.arrivals:
            arrival.wait_recv()
        self.keep.finish()
        for copy in self.copies:
            copy.wait_send()


def far_peers(s, c, ny):
    return [((s // TP + j) % ny * TP + s % TP, c) for j in range(1, ny)]


class RowSum:
    def __init__(self, parts, out, part, core, far, send, recv, local_sem, s, c, rank):
        self.out, self.part, self.core, self.far, self.at = out, part, core, far, (s, c)
        self.send, self.recv, self.local_sem = send, recv, local_sem
        self.copies, self.loads = {}, {}
        for d in (2, 0):
            copy = remote(
                parts.at[flip(rank, d + 1)],
                core.at[d // 2],
                send.at[d // 2],
                recv.at[d // 2],
                (flip(s, 1), c),
            )
            copy.start()
            self.copies[d] = copy
            self.loads[d] = pltpu.make_async_copy(
                parts.at[flip(rank, d)], part.at[d // 2], local_sem.at[d // 2]
            )
            self.loads[d].start()

    def forward(self):
        s, c = self.at
        rows = self.part.shape[1]
        for d in (2, 0):
            self.loads[d].wait()
            self.copies[d].wait_recv()
            add_into(self.part.at[d // 2], self.core.at[d // 2], rows)
            if d == 2:
                copy = remote(
                    self.part.at[1], self.far, self.send.at[2], self.recv.at[2], (flip(s, 2), c)
                )
                copy.start()
                self.copies[3] = copy

    def finish(self):
        self.copies[3].wait_recv()
        add_into(self.part.at[0], self.far, self.part.shape[1])
        write = pltpu.make_async_copy(self.part.at[0], self.out, self.local_sem.at[2])
        write.start()
        for copy in self.copies.values():
            copy.wait_send()
        write.wait()


def quad_here():
    s, c = lax.axis_index("shard"), lax.axis_index("ctx")
    return s, c, s % TP


def first_kernel(ns, *refs):
    parts, small, passed, wide, all_small, passed_on = refs[:2], *refs[2:4], refs[4:6], *refs[6:8]
    send, recv, send_small, recv_small, local_sem = refs[8:13]
    rooms, small_room, passed_room = refs[13:15], *refs[15:]
    s, c, rank = quad_here()
    others = [((s + j) % ns, c) for j in range(1, ns)]
    greet(others)
    copies = []
    for j in range(1, ns):
        copy = remote(
            small, all_small.at[s], send_small.at[j - 1], recv_small.at[j - 1], others[j - 1]
        )
        copy.start()
        copies.append(copy)
    two = Parts(parts, wide, send, recv, rooms, local_sem, s, c, rank)
    own = Keep(small, all_small.at[s], small_room, local_sem.at[2])
    kept = Keep(passed, passed_on, passed_room, local_sem.at[3])
    own.forward()
    kept.forward()
    two.forward()
    for j in range(1, ns):
        block = all_small.at[(s + ns - j) % ns]
        remote(block, block, send_small.at[j - 1], recv_small.at[j - 1], (s, c)).wait_recv()
    two.finish()
    own.finish()
    kept.finish()
    for copy in copies:
        copy.wait_send()


def first_exchange(parts, small, passed, ns):
    any_spec = pl.BlockSpec(memory_space=pl.ANY)
    return pl.pallas_call(
        functools.partial(first_kernel, ns),
        out_shape=[jax.ShapeDtypeStruct(p.shape, BF) for p in parts]
        + [
            jax.ShapeDtypeStruct((ns,) + small.shape, BF),
            jax.ShapeDtypeStruct(passed.shape, BF),
        ],
        in_specs=[any_spec] * 4,
        out_specs=[any_spec] * 4,
        scratch_shapes=[
            pltpu.SemaphoreType.DMA((2, TP)),
            pltpu.SemaphoreType.DMA((2, TP)),
            pltpu.SemaphoreType.DMA((ns - 1,)),
            pltpu.SemaphoreType.DMA((ns - 1,)),
            pltpu.SemaphoreType.DMA((4, 2)),
        ]
        + [pltpu.VMEM(p.shape[1:], BF) for p in parts]
        + [pltpu.VMEM(x.shape, BF) for x in (small, passed)],
        compiler_params=pltpu.CompilerParams(collective_id=5, has_side_effects=True),
        cost_estimate=exchange_cost(25),
        name="first_exchange",
    )(*parts, small, passed)


def share_scratch(weight, act, ny):
    return [
        pltpu.SemaphoreType.DMA((ny - 1,)),
        pltpu.SemaphoreType.DMA((ny - 1,)),
        pltpu.SemaphoreType.DMA((TP,)),
        pltpu.SemaphoreType.DMA((TP,)),
        pltpu.SemaphoreType.DMA((2, 2)),
        pltpu.VMEM(weight.shape, BF),
        pltpu.VMEM(act.shape, BF),
    ]


def hidden_kernel(ny, weight, act, fc_hbm, cot_hbm, bias, wide, act_out, g_out, slope_out, proj_out, *refs):
    acts, w_fc, cot, bent, slope, grad_proj = refs[:6]
    send_far, recv_far, send, recv, far_sem, load_sem, out_sem, room = refs[6:]
    s, c, rank = quad_here()
    rows = acts.shape[1]
    loads = [
        pltpu.make_async_copy(src, dst, load_sem.at[i])
        for i, (src, dst) in enumerate(((act, acts.at[rank]), (fc_hbm, w_fc), (cot_hbm, cot)))
    ]
    for load in loads:
        load.start()
    greet([(flip(s, d), c) for d in (1, 2)] + far_peers(s, c, ny))
    far = Far(weight, wide, send_far, recv_far, room, far_sem, s, c, ny)
    loads[0].wait()
    copies = []

    def push(d):
        hop = 2 if d == 2 else 1
        block = acts.at[flip(rank, d - hop)]
        copy = remote(block, block, send.at[d], recv.at[d], (flip(s, hop), c))
        copy.start()
        copies.append(copy)

    def arrived(d):
        block = acts.at[flip(rank, d)]
        remote(block, block, send.at[d], recv.at[d], (s, c)).wait_recv()

    push(2)
    push(1)
    loads[1].wait()
    far.forward()

    def hidden(d):
        block = flip(rank, d)

        def step(i, carry):
            at = pl.ds(pl.multiple_of(i * 128, 128), 128)
            h = mm(acts[block, at, :], w_fc[...], NN) + bias[...]
            tanh = jnp.tanh(0.7978845608028654 * (h + 0.044715 * h * h * h))
            to = pl.ds(pl.multiple_of(block * rows + i * 128, 128), 128)
            bent[to, :] = (0.5 * h * (1.0 + tanh)).astype(BF)
            slope[to, :] = 0.5 * (1.0 + tanh) + 0.5 * h * (
                1.0 - tanh * tanh
            ) * 0.7978845608028654 * (1.0 + 3.0 * 0.044715 * h * h)
            return carry

        lax.fori_loop(0, rows // 128, step, 0)

    hidden(0)
    arrived(1)
    hidden(1)
    arrived(2)
    push(3)
    hidden(2)
    arrived(3)
    writes = [
        pltpu.make_async_copy(acts.at[t], act_out.at[t], out_sem.at[t]) for t in range(TP)
    ]
    for write in writes:
        write.start()
    hidden(3)
    more = [
        pltpu.make_async_copy(bent, g_out, out_sem.at[TP]),
        pltpu.make_async_copy(slope, slope_out, out_sem.at[TP + 1]),
    ]
    for write in more:
        write.start()
    loads[2].wait()
    width = bent.shape[1]

    def proj_step(i, carry):
        at = pl.ds(pl.multiple_of(i * 256, 256), 256)
        grad_proj[at, :] = mm(bent[:, at], cot[...], TN).astype(BF)
        return carry

    lax.fori_loop(0, width // 256, proj_step, 0)
    if width % 256:
        at = pl.ds(width // 256 * 256, width % 256)
        grad_proj[at, :] = mm(bent[:, at], cot[...], TN).astype(BF)
    more.append(pltpu.make_async_copy(grad_proj, proj_out, out_sem.at[TP + 2]))
    more[-1].start()
    far.finish()
    for copy in copies:
        copy.wait_send()
    for write in writes + more:
        write.wait()


def hidden_rows(weight, act, w_fc, cot, bias, ny):
    any_spec = pl.BlockSpec(memory_space=pl.ANY)
    rows, width = act.shape
    hq = w_fc.shape[1]
    return pl.pallas_call(
        functools.partial(hidden_kernel, ny),
        out_shape=[
            jax.ShapeDtypeStruct((ny,) + weight.shape, BF),
            jax.ShapeDtypeStruct((TP, rows, width), BF),
            jax.ShapeDtypeStruct((TP * rows, hq), BF),
            jax.ShapeDtypeStruct((TP * rows, hq), F32),
            jax.ShapeDtypeStruct((hq, cot.shape[1]), BF),
        ],
        in_specs=[any_spec] * 4 + [pl.BlockSpec(memory_space=pltpu.VMEM)],
        out_specs=[any_spec] * 5,
        scratch_shapes=[
            pltpu.VMEM((TP, rows, width), BF),
            pltpu.VMEM(w_fc.shape, BF),
            pltpu.VMEM(cot.shape, BF),
            pltpu.VMEM((TP * rows, hq), BF),
            pltpu.VMEM((TP * rows, hq), F32),
            pltpu.VMEM((hq, cot.shape[1]), BF),
            pltpu.SemaphoreType.DMA((ny - 1,)),
            pltpu.SemaphoreType.DMA((ny - 1,)),
            pltpu.SemaphoreType.DMA((TP,)),
            pltpu.SemaphoreType.DMA((TP,)),
            pltpu.SemaphoreType.DMA((2,)),
            pltpu.SemaphoreType.DMA((3,)),
            pltpu.SemaphoreType.DMA((TP + 3,)),
            pltpu.VMEM(weight.shape, BF),
        ],
        compiler_params=pltpu.CompilerParams(
            collective_id=3, has_side_effects=True, vmem_limit_bytes=VMEM_BYTES
        ),
        cost_estimate=exchange_cost(60),
        name="hidden_rows",
    )(weight, act, w_fc, cot, bias)


def sum_scratch(act):
    return [
        pltpu.VMEM((2,) + act, BF),
        pltpu.VMEM((2,) + act, BF),
        pltpu.VMEM(act, BF),
        pltpu.SemaphoreType.DMA((3,)),
        pltpu.SemaphoreType.DMA((3,)),
        pltpu.SemaphoreType.DMA((3,)),
    ]


def add_rows(target, other):
    def step(i, carry):
        rows = pl.ds(pl.multiple_of(i * 16, 16), 16)
        target[rows] = (target[rows].astype(F32) + other[rows].astype(F32)).astype(BF)
        return carry

    lax.fori_loop(0, target.shape[0] // 16, step, 0)


def middle_kernel(*refs):
    grad_hbm, fc_hbm, act_hbm, proj_hbm, in_hbm = refs[:5]
    sum_out, out_out, fc_out = refs[5:8]
    grad, w_fc, act, w_proj, act_in, out_part, grad_fc = refs[8:15]
    parts, core, far = refs[15:18]
    send, recv, load_sem, out_sem = refs[18:]
    s, c, rank = quad_here()
    loads = [
        pltpu.make_async_copy(src, dst, load_sem.at[i])
        for i, (src, dst) in enumerate(
            (
                (grad_hbm, grad),
                (fc_hbm, w_fc),
                (act_hbm, act),
                (proj_hbm, w_proj),
                (in_hbm, act_in),
            )
        )
    ]
    for load in loads:
        load.start()
    greet([(flip(s, d), c) for d in (1, 2)])
    rows = far.shape[0]
    loads[0].wait()
    loads[1].wait()

    def part(d):
        block = grad[pl.ds(pl.multiple_of(flip(rank, d) * rows, rows), rows), :]
        parts[d] = mm(block, w_fc[...], NT).astype(BF)

    copies = {}
    for d in (3, 1):
        part(d)
        copy = remote(
            parts.at[d], core.at[d // 2], send.at[d // 2], recv.at[d // 2], (flip(s, 1), c)
        )
        copy.start()
        copies[d] = copy
    part(2)
    copies[3].wait_recv()
    add_rows(parts.at[2], core.at[1])
    across = remote(parts.at[2], far, send.at[2], recv.at[2], (flip(s, 2), c))
    across.start()
    part(0)
    copies[1].wait_recv()
    add_rows(parts.at[0], core.at[0])
    loads[2].wait()
    loads[3].wait()
    step_rows = 256 if act.shape[0] % 256 == 0 else 128

    def out_step(i, carry):
        at = pl.ds(pl.multiple_of(i * step_rows, step_rows), step_rows)
        out_part[at, :] = mm(act[at, :], w_proj[...], NN).astype(BF)
        return carry

    lax.fori_loop(0, act.shape[0] // step_rows, out_step, 0)
    writes = [pltpu.make_async_copy(out_part, out_out, out_sem.at[0])]
    writes[0].start()
    loads[4].wait()
    width = act_in.shape[1]

    def fc_step(i, carry):
        at = pl.ds(pl.multiple_of(i * 256, 256), 256)
        grad_fc[at, :] = mm(act_in[:, at], grad[...], TN).astype(BF)
        return carry

    lax.fori_loop(0, width // 256, fc_step, 0)
    if width % 256:
        at = pl.ds(width // 256 * 256, width % 256)
        grad_fc[at, :] = mm(act_in[:, at], grad[...], TN).astype(BF)
    writes.append(pltpu.make_async_copy(grad_fc, fc_out, out_sem.at[1]))
    writes[1].start()
    across.wait_recv()
    add_rows(parts.at[0], far)
    writes.append(pltpu.make_async_copy(parts.at[0], sum_out, out_sem.at[2]))
    writes[2].start()
    for copy in copies.values():
        copy.wait_send()
    across.wait_send()
    for write in writes:
        write.wait()


def middle_rows(grad, w_fc, act, w_proj, act_in):
    any_spec = pl.BlockSpec(memory_space=pl.ANY)
    rows = grad.shape[0] // TP
    width = act_in.shape[1]
    return pl.pallas_call(
        middle_kernel,
        out_shape=[
            jax.ShapeDtypeStruct((rows, width), BF),
            jax.ShapeDtypeStruct((TP * rows, w_proj.shape[1]), BF),
            jax.ShapeDtypeStruct((width, grad.shape[1]), BF),
        ],
        in_specs=[any_spec] * 5,
        out_specs=[any_spec] * 3,
        scratch_shapes=[pltpu.VMEM(x.shape, BF) for x in (grad, w_fc, act, w_proj, act_in)]
        + [
            pltpu.VMEM((TP * rows, w_proj.shape[1]), BF),
            pltpu.VMEM((width, grad.shape[1]), BF),
            pltpu.VMEM((TP, rows, width), BF),
            pltpu.VMEM((2, rows, width), BF),
            pltpu.VMEM((rows, width), BF),
            pltpu.SemaphoreType.DMA((3,)),
            pltpu.SemaphoreType.DMA((3,)),
            pltpu.SemaphoreType.DMA((5,)),
            pltpu.SemaphoreType.DMA((3,)),
        ],
        compiler_params=pltpu.CompilerParams(
            collective_id=4, has_side_effects=True, vmem_limit_bytes=VMEM_BYTES
        ),
        cost_estimate=exchange_cost(50),
        name="middle_rows",
    )(grad, w_fc, act, w_proj, act_in)


def last_kernel(*refs):
    parts, wide = refs[:2], refs[3:5]
    send, recv, local_sem = refs[5:8]
    s, c, rank = quad_here()
    greet([(flip(s, d), c) for d in (1, 2, 3)])
    two = Parts(parts, wide, send, recv, refs[8:], local_sem, s, c, rank)
    two.forward()
    two.finish()


def last_exchange(parts, ready):
    any_spec = pl.BlockSpec(memory_space=pl.ANY)
    return pl.pallas_call(
        last_kernel,
        out_shape=[jax.ShapeDtypeStruct(p.shape, BF) for p in parts],
        in_specs=[any_spec] * 3,
        out_specs=[any_spec] * 2,
        scratch_shapes=[
            pltpu.SemaphoreType.DMA((2, TP)),
            pltpu.SemaphoreType.DMA((2, TP)),
            pltpu.SemaphoreType.DMA((2, 2)),
        ]
        + [pltpu.VMEM(p.shape[1:], BF) for p in parts],
        compiler_params=pltpu.CompilerParams(collective_id=6, has_side_effects=True),
        cost_estimate=exchange_cost(20),
        name="last_exchange",
    )(*parts, ready)


NN = (((1,), (0,)), ((), ()))
NT = (((1,), (1,)), ((), ()))
TN = (((0,), (0,)), ((), ()))


def mm(left, right, dims):
    return lax.dot_general(left, right, dims, preferred_element_type=F32)


def halves(rows):
    lane = lax.broadcasted_iota(jnp.int32, (rows, 2 * HD), 1)
    return lane < HD


def one_of(values, low, head):
    return jnp.where(low if head == 0 else jnp.logical_not(low), values, jnp.zeros_like(values))


def for_pairs(width, body, between):
    pairs = width // (2 * HD)

    def step(i, carry):
        body(pl.ds(pl.multiple_of(i * 2 * HD, 2 * HD), 2 * HD), 2 * i, 2)
        return carry

    start = 0
    for n, extra in enumerate(between):
        stop = pairs * (n + 1) // (len(between) + 1)
        lax.fori_loop(start, stop, step, 0)
        extra()
        start = stop
    lax.fori_loop(start, pairs, step, 0)
    if width % (2 * HD):
        body(pl.ds(pairs * 2 * HD, HD), 2 * pairs, 1)


def attend_kernel(ny, *refs):
    q_ref, k_ref, v_ref, bias_ref, weight, act = refs[:6]
    o_ref, lse_ref, wide, wide_act, token = refs[6:11]
    send_far, recv_far, send_act, recv_act, local_sem, room, act_room = refs[11:]
    token[0] = jnp.int32(0)
    width = q_ref.shape[1]
    low = halves(k_ref.shape[0])
    s, c, rank = quad_here()
    greet([(flip(s, d), c) for d in (1, 2)] + far_peers(s, c, ny))
    far = Far(weight, wide, send_far, recv_far, room, local_sem.at[1], s, c, ny)
    rows = Share(act, wide_act, send_act, recv_act, act_room, local_sem.at[0], s, c, rank)

    def body(cols, first, count):
        q = q_ref[:, cols]
        k = k_ref[:, cols]
        v = v_ref[:, cols]
        total = None
        for head in range(count):
            k_h = one_of(k, low, head) if count == 2 else k
            v_h = one_of(v, low, head) if count == 2 else v
            scores = mm(q, k_h, NT) + bias_ref[...]
            peak = jnp.max(scores, axis=1, keepdims=True)
            weights = jnp.exp(scores - peak)
            norm = jnp.sum(weights, axis=1, keepdims=True)
            part = mm(weights.astype(BF), v_h, NN) / norm
            total = part if total is None else total + part
            lse_ref[first + head] = peak + jnp.log(norm)
        o_ref[:, cols] = total.astype(BF)

    for_pairs(width, body, [far.forward, lambda: None, lambda: None])
    rows.forward()
    rows.finish()
    far.finish()


def attend_forward(q, k, v, bias, weight, act, ny):
    heads = q.shape[1] // HD
    vmem = pl.BlockSpec(memory_space=pltpu.VMEM)
    any_spec = pl.BlockSpec(memory_space=pl.ANY)
    return pl.pallas_call(
        functools.partial(attend_kernel, ny),
        out_shape=[
            jax.ShapeDtypeStruct(q.shape, BF),
            jax.ShapeDtypeStruct((heads, q.shape[0], 1), F32),
            jax.ShapeDtypeStruct((ny,) + weight.shape, BF),
            jax.ShapeDtypeStruct((TP,) + act.shape, BF),
            jax.ShapeDtypeStruct((1,), jnp.int32),
        ],
        in_specs=[vmem] * 4 + [any_spec] * 2,
        out_specs=[vmem] * 2 + [any_spec] * 2 + [pl.BlockSpec(memory_space=pltpu.SMEM)],
        scratch_shapes=share_scratch(weight, act, ny),
        compiler_params=pltpu.CompilerParams(
            collective_id=7, has_side_effects=True, vmem_limit_bytes=VMEM_BYTES
        ),
        cost_estimate=exchange_cost(60),
        name="attend_forward",
    )(q, k, v, bias, weight, act)


def attend_back_kernel(*refs):
    q_ref, k_ref, v_ref, g_ref, lse_ref, bias_ref, _, parts = refs[:8]
    dq_ref, dk_ref, dv_ref, out = refs[8:12]
    width = q_ref.shape[1]
    low_q = halves(q_ref.shape[0])
    low_k = halves(k_ref.shape[0])
    scale = 1.0 / math.sqrt(HD)
    s, c, rank = quad_here()
    greet([(flip(s, d), c) for d in (1, 2)])
    rows = RowSum(parts, out, *refs[12:], s, c, rank)

    def body(cols, first, count):
        q = q_ref[:, cols]
        k = k_ref[:, cols]
        v = v_ref[:, cols]
        g = g_ref[:, cols]
        dq = dk = dv = None
        for head in range(count):
            if count == 2:
                q_h, g_h = one_of(q, low_q, head), one_of(g, low_q, head)
                k_h = one_of(k, low_k, head)
            else:
                q_h, g_h, k_h = q, g, k
            scores = mm(k, q_h, NT) + bias_ref[...]
            probs = jnp.exp(scores - lse_ref[first + head])
            grad = mm(v, g_h, NT)
            both = probs * grad
            centre = jnp.sum(both, axis=0, keepdims=True)
            ds = (both - probs * centre).astype(BF)
            dq_h = mm(ds, k_h, TN)
            dk_h = mm(ds, q_h, NN)
            dv_h = mm(probs.astype(BF), g_h, NN)
            dq = dq_h if dq is None else dq + dq_h
            dk = dk_h if dk is None else dk + dk_h
            dv = dv_h if dv is None else dv + dv_h
        dq_ref[:, cols] = (dq * scale).astype(BF)
        dk_ref[:, cols] = dk.astype(BF)
        dv_ref[:, cols] = dv.astype(BF)

    for_pairs(width, body, [rows.forward, lambda: None, lambda: None])
    rows.finish()


def attend_backward(q, k, v, g, lse, bias, ready, parts):
    vmem = pl.BlockSpec(memory_space=pltpu.VMEM)
    any_spec = pl.BlockSpec(memory_space=pl.ANY)
    act = parts.shape[1:]
    return pl.pallas_call(
        attend_back_kernel,
        out_shape=[jax.ShapeDtypeStruct(x.shape, BF) for x in (q, k, v)]
        + [jax.ShapeDtypeStruct(act, BF)],
        in_specs=[vmem] * 6 + [any_spec] * 2,
        out_specs=[vmem] * 3 + [any_spec],
        scratch_shapes=sum_scratch(act),
        compiler_params=pltpu.CompilerParams(
            collective_id=8, has_side_effects=True, vmem_limit_bytes=VMEM_BYTES
        ),
        cost_estimate=exchange_cost(47),
        name="attend_backward",
    )(q, k, v, g, lse, bias, ready, parts)


def normed(values):
    mean = jnp.mean(values, axis=-1, keepdims=True)
    centred = values - mean
    spread = jnp.mean(centred * centred, axis=-1, keepdims=True)
    inverse = lax.rsqrt(spread + NORM_EPS)
    return centred * inverse, inverse


def norm_back(u, unit, inverse, gain):
    gu = gain * u
    grad = inverse * (
        gu - jnp.mean(gu, axis=-1, keepdims=True) - unit * jnp.mean(gu * unit, axis=-1, keepdims=True)
    )
    return grad, jnp.sum(u * unit, axis=0), jnp.sum(u, axis=0)


def adamw(master, first, second, gradient, rate, decay):
    first_new = BETA_ONE * first + (1.0 - BETA_ONE) * gradient
    second_new = BETA_TWO * second + (1.0 - BETA_TWO) * gradient * gradient
    fix_one = 1.0 - BETA_ONE**STEP
    fix_two = 1.0 - BETA_TWO**STEP
    update = first_new / fix_one / (jnp.sqrt(second_new / fix_two) + ADAM_EPS)
    master_new = master - rate * (update + decay * master)
    return (master_new, first_new, second_new, master_new.astype(BF))


def cuts(start, stop, width):
    found = []
    while start < stop:
        block, low = divmod(start, width)
        high = min(width, low + stop - start)
        found.append((block, low, high))
        start += high - low
    return found


def after(first, later):
    return lax.optimization_barrier((first, later))[1]


def behind(token, value):
    return jnp.where(token[0] == 0, value, jnp.zeros_like(value))


def local(
    tokens,
    cotangent,
    master_qkv,
    master_out,
    master_fc,
    master_proj,
    master_small,
    first_qkv,
    first_out,
    first_fc,
    first_proj,
    first_small,
    second_qkv,
    second_out,
    second_fc,
    second_proj,
    second_small,
):
    ns, nc = lax.axis_size("shard"), lax.axis_size("ctx")
    s, c = lax.axis_index("shard"), lax.axis_index("ctx")
    ny = ns // TP
    rank = s % TP
    rows = tokens.shape[0]
    prompt_rows = PROMPT // nc
    kr = D // ns
    hs = FF // ns // TP
    hq = ns * hs
    hc = hq // nc
    oc = D // nc
    pack = 8 if kr % 8 == 0 else 4
    packed = (kr // pack, pack, D)
    act_pack = (rows // 8, 8, D)
    far_groups = [[y * TP + r for y in range(ny)] for r in range(TP)]

    qc = master_qkv.shape[1]
    attn_block = jnp.concatenate([master_qkv.astype(BF), master_out.astype(BF)], axis=1)
    attn_z = lax.all_gather(attn_block, "ctx", axis=0)
    fc_parts = master_fc.astype(BF).reshape(kr, ns // nc, TP, hs).transpose(2, 0, 1, 3)
    proj_parts = master_proj.astype(BF).reshape(TP, hs, D // nc)
    fc_quad, proj_quad, small_all, prompt_own = first_exchange(
        [fc_parts.reshape(TP, kr, hc), proj_parts],
        master_small.astype(BF),
        tokens[:prompt_rows],
        ns,
    )
    small = small_all.transpose(1, 0, 2).reshape(master_small.shape[0], D).astype(F32)
    prompt_tokens = lax.all_gather(prompt_own, "ctx", axis=0, tiled=True)
    fc_z = lax.all_gather(after(attn_z, fc_quad), "ctx", axis=0)
    proj_z = lax.all_gather(after(attn_z, proj_quad), "ctx", axis=0)

    qkv_rows = [
        jnp.concatenate(
            [attn_z[b, :, low:high] for b, low, high in cuts(i * D, (i + 1) * D, qc)], axis=1
        )
        for i in range(3)
    ]
    out_rows = jnp.concatenate([attn_z[b, :, qc:] for b in range(nc)], axis=1)
    gathered = gather_rows([w.reshape(packed) for w in qkv_rows + [out_rows]], ns)
    w_q, w_k, w_v, w_o = [w.reshape(D, D) for w in gathered[:4]]
    fc_z = behind(gathered[4], fc_z).reshape(nc, TP * kr, hc)
    fc_rows = jnp.concatenate([fc_z[b] for b in range(nc)], axis=1)

    own = tokens.astype(F32)
    unit_one, inverse_one = normed(own)
    all_rows = jnp.concatenate([prompt_tokens, tokens[prompt_rows:]], axis=0).astype(F32)
    unit_all = normed(all_rows)[0]
    act_all = (unit_all * small[0] + small[1]).astype(BF)
    act_one = jnp.concatenate(
        [lax.dynamic_slice_in_dim(act_all, c * prompt_rows, prompt_rows), act_all[PROMPT:]], axis=0
    )
    scale = 1.0 / math.sqrt(HD)
    q = (mm(act_one, w_q, NN) + small[4]).astype(BF) * BF(scale)
    k = mm(act_all, w_k, NN).astype(BF)
    v = (mm(act_all, w_v, NN) + small[5]).astype(BF)
    places = jnp.arange(rows, dtype=jnp.int32)
    in_prompt = places < prompt_rows
    later = places - prompt_rows
    pos_query = jnp.where(in_prompt, c * prompt_rows + places, PROMPT + later % BLK)
    seq_query = jnp.where(in_prompt, -1, later // BLK)
    cont_keys = jnp.arange(rows - prompt_rows, dtype=jnp.int32)
    pos_key = jnp.concatenate([jnp.arange(PROMPT, dtype=jnp.int32), PROMPT + cont_keys % BLK])
    seq_key = jnp.concatenate([jnp.full((PROMPT,), -1, jnp.int32), cont_keys // BLK])
    allowed = (pos_key[None, :] <= pos_query[:, None]) & (
        (seq_key[None, :] == -1) | (seq_key[None, :] == seq_query[:, None])
    )
    bias = jnp.where(allowed, 0.0, MASKED).astype(F32)
    attended, log_totals, w_fc, cot_wide, token = attend_forward(
        q, k, v, bias, fc_rows.reshape(TP * packed[0], pack, hq), cotangent.reshape(act_pack), ny
    )
    middle = own + mm(attended, w_o, NN) + small[6]
    unit_two, inverse_two = normed(middle)
    act_two = (unit_two * small[2] + small[3]).astype(BF)

    proj_z = behind(token, proj_z).reshape(nc, TP * hs, oc)
    proj_rows = jnp.concatenate([proj_z[b] for b in range(nc)], axis=1)
    pack_hs = 8 if hs % 8 == 0 else 4
    w_fc = w_fc.reshape(D, hq)
    cot_wide = cot_wide.reshape(TP * rows, D)
    fc_bias = lax.dynamic_index_in_dim(
        small[7 : 7 + FF // D].reshape(ns, TP, hs), rank, axis=1, keepdims=False
    ).reshape(1, hq)
    w_proj, act_wide, act_three, slope, grad_proj = hidden_rows(
        proj_rows.reshape(TP * hs // pack_hs, pack_hs, D), act_two, w_fc, cot_wide, fc_bias, ny
    )
    w_proj = w_proj.reshape(hq, D)
    act_wide = act_wide.reshape(TP * rows, D)
    proj_far = lax.psum_scatter(
        grad_proj, "shard", scatter_dimension=0, tiled=True, axis_index_groups=far_groups
    )
    grad_hidden = (mm(cot_wide, w_proj, NT) * slope).astype(BF)
    mid_sum, out_part, grad_fc = middle_rows(grad_hidden, w_fc, act_three, w_proj, act_wide)
    grad_fc_bias = jnp.sum(grad_hidden, axis=0, dtype=F32)
    fc_far = lax.psum_scatter(
        grad_fc, "shard", scatter_dimension=0, tiled=True, axis_index_groups=far_groups
    )
    proj_far = proj_far.reshape(TP * hs, nc, D // nc).transpose(1, 0, 2)
    proj_near = lax.psum_scatter(proj_far, "ctx", scatter_dimension=0)
    fc_far = fc_far.reshape(TP * kr, nc, hc).transpose(1, 0, 2)
    fc_near = lax.psum_scatter(fc_far, "ctx", scatter_dimension=0)

    grad_output = cotangent.astype(F32)
    grad_norm, gain_two, shift_two = norm_back(
        mid_sum.astype(F32), unit_two, inverse_two, small[2]
    )
    grad_middle = grad_output + grad_norm
    grad_branch = grad_middle.astype(BF)
    grad_wo = mm(attended, grad_branch, TN).astype(BF)
    grad_attended = mm(grad_branch, w_o, NT).astype(BF)
    grad_q, grad_k, grad_v, out_sum = attend_backward(
        q, k, v, grad_attended, log_totals.transpose(0, 2, 1), bias.T, proj_far,
        out_part.reshape((TP,) + act_pack),
    )
    output = middle + out_sum.reshape(rows, D).astype(F32) + small[small.shape[0] - 1]
    key_part = mm(grad_k, w_k, NT) + mm(grad_v, w_v, NT)
    prompt_sum = lax.psum_scatter(
        key_part[:PROMPT].astype(BF), "ctx", scatter_dimension=0, tiled=True
    )
    query_part = mm(grad_q, w_q, NT)
    grad_wq = mm(act_one, grad_q, TN).astype(BF)
    grad_wk = mm(act_all, grad_k, TN).astype(BF)
    grad_wv = mm(act_all, grad_v, TN).astype(BF)

    hidden_grads = lax.dynamic_update_index_in_dim(
        jnp.zeros((ns, TP, hs), F32), grad_fc_bias.reshape(ns, 1, hs), rank, axis=1
    )
    small_grads = jnp.concatenate(
        [
            jnp.stack(
                [
                    jnp.sum(key_part * unit_all, axis=0) + jnp.sum(query_part * unit_one, axis=0),
                    jnp.sum(key_part, axis=0) + jnp.sum(query_part, axis=0),
                    gain_two,
                    shift_two,
                    jnp.sum(grad_q, axis=0, dtype=F32),
                    jnp.sum(grad_v, axis=0, dtype=F32),
                    jnp.sum(grad_branch, axis=0, dtype=F32),
                ]
            ),
            hidden_grads.reshape(FF // D, D),
            jnp.sum(grad_output, axis=0)[None],
        ],
        axis=0,
    )
    n_small = small_grads.shape[0]
    small_parts = small_grads.reshape(n_small, ns, kr).transpose(1, 0, 2).reshape(ns, n_small * kr)
    small_parts = jnp.pad(small_parts, ((0, 0), (0, 8 * D - n_small * kr)))
    back_q, back_k, back_v, back_o, back_small = scatter_rows(
        [g.reshape((ns,) + packed) for g in (grad_wq, grad_wk, grad_wv, grad_wo)]
        + [small_parts.astype(BF).reshape(ns, 1, 8, D)],
        ns,
    )
    fc_back, proj_back = last_exchange(
        [fc_near.reshape(TP, kr, hc), proj_near.reshape(TP, hs, D // nc)], back_small
    )
    qkv_back = [b.reshape(kr, D) for b in (back_q, back_k, back_v)]
    back_o = back_o.reshape(kr, D)
    attn_back = jnp.stack(
        [
            jnp.concatenate(
                [qkv_back[i][:, low:high] for i, low, high in cuts(b * qc, (b + 1) * qc, D)]
                + [back_o[:, b * oc : (b + 1) * oc]],
                axis=1,
            )
            for b in range(nc)
        ]
    )
    wide_rows = attn_back.shape[2]
    small_back = back_small.reshape(8 * D)[: 8 * wide_rows].reshape(1, 8, wide_rows)
    grad_attn = lax.psum_scatter(
        jnp.concatenate([attn_back, jnp.broadcast_to(small_back, (nc, 8, wide_rows))], axis=1),
        "ctx",
        scatter_dimension=0,
    )
    small_own = grad_attn[kr:].reshape(-1)[: n_small * kr].reshape(n_small, kr).astype(F32)
    grad_act = query_part + jnp.concatenate(
        [prompt_sum.astype(F32), key_part[PROMPT:]], axis=0
    )
    grad_norm, _, _ = norm_back(grad_act, unit_one, inverse_one, small[0])
    grad_input = grad_middle + grad_norm

    gradients = (
        grad_attn[:kr, :qc].astype(F32),
        grad_attn[:kr, qc:].astype(F32),
        fc_back.reshape(TP, kr, ns // nc, hs).transpose(1, 2, 0, 3).reshape(kr, FF // nc).astype(F32),
        proj_back.reshape(TP * hs, D // nc).astype(F32),
        small_own,
    )
    masters = (master_qkv, master_out, master_fc, master_proj, master_small)
    firsts = (first_qkv, first_out, first_fc, first_proj, first_small)
    seconds = (second_qkv, second_out, second_fc, second_proj, second_small)
    rates = (D ** (-0.5), max(D // 256, 1) ** (-0.5), D ** (-0.5), FF ** (-0.5), SMALL_RATE)
    decays = (WEIGHT_DECAY, WEIGHT_DECAY, WEIGHT_DECAY, WEIGHT_DECAY, 0.0)
    results = [
        adamw(masters[i], firsts[i], seconds[i], gradients[i], rates[i], decays[i]) for i in range(5)
    ]
    return (output.astype(BF), grad_input) + tuple(results[i][j] for j in range(4) for i in range(5))


def solution(mesh):
    row_spec = P(("shard", "ctx"), None)
    weight_specs = (P("shard", "ctx"),) * 4 + (P(None, "shard"),)
    return jax.shard_map(
        local,
        mesh=mesh,
        in_specs=(row_spec, row_spec) + weight_specs * 3,
        out_specs=(row_spec, row_spec) + weight_specs * 4,
        check_vma=False,
    )
```
